128 devices in a mesh: shard: 16 (over z, y_lo, core), replica: 8 (over x, y_hi).
Axes of the slice: x: 4, y: 4 (y_hi: 2, y_lo: 2; y = y_hi * 2 + y_lo), z: 4, core: 2. Of those that a mesh axis runs over, the one named last changes fastest.
Arguments:
- tokens: bfloat16 [24576, 1024], P(('shard', 'replica')), may hold values from -6 to 6
- norm_one: bfloat16 [1024], P('shard'), may hold values from 0.5 to 1.5
- query_weight: bfloat16 [1024, 1024], P('shard'), may hold values from -0.1875 to 0.1875
- key_matrix: bfloat16 [1024, 512], P('shard'), may hold values from -0.1875 to 0.1875
- value_matrix: bfloat16 [1024, 512], P('shard'), may hold values from -0.1875 to 0.1875
- out_weight: bfloat16 [1024, 1024], P('shard'), may hold values from -1.5 to 1.5
- norm_two: bfloat16 [1024], P('shard'), may hold values from 0.5 to 1.5
- router: bfloat16 [1024, 32], P('shard'), may hold values from -0.09375 to 0.09375
- experts: bfloat16 [32, 3, 1024, 512], P('shard'), may hold values from -4 to 4
- routes: int32 [24576, 8], P(('shard', 'replica')), may hold values from 0 to 31, all different within a row; in each aligned block of 192 rows (0 to 191, 192 to 383, ...) at most 60 rows name the same one
- segments: int32 [24576], P(('shard', 'replica')), may hold values from 0 to 47, as said below
- cotangent: bfloat16 [24576, 1024], P(('shard', 'replica')), may hold values from -6 to 6
Outputs:
- layer_out: bfloat16 [24576, 1024], P(('shard', 'replica'))
- grad_tokens: bfloat16 [24576, 1024], P(('shard', 'replica'))
- grad_norm_one: float32 [1024], P('shard')
- grad_query: float32 [1024, 1024], P('shard')
- grad_key: float32 [1024, 512], P('shard')
- grad_value: float32 [1024, 512], P('shard')
- grad_out_weight: float32 [1024, 1024], P('shard')
- grad_norm_two: float32 [1024], P('shard')
- grad_router: float32 [1024, 32], P('shard')
- grad_experts: float32 [32, 3, 1024, 512], P('shard')
The draws below stay inside these ranges and needn't reach their ends.
Inputs may be any that keep to these rules, and one draw needn't show every extreme that they name: `routes`: each row names 8 different experts; among the 192 rows of one device no expert is named by more than 60 rows. `segments`: segment numbers never fall. Sequence s (tokens s * 1536 to (s + 1) * 1536 - 1) holds documents 3 s, 3 s + 1 and 3 s + 2, none empty; document 3 s + 1 begins within the first 192 tokens of its sequence and ends within the last 192.
All inputs are finite; a program needn't handle non-finite values.
Results may differ from the reference program's by a relative error of at most 0.025.
Values may be sent and summed in bfloat16 or wider, within the bound.
No kernel may reach another device: no remote copies, remote signals or barrier semaphores. Data moves between devices by JAX's collectives and lax.ppermute only.
A program may use at most 192 MiB of HBM per device.

```python
import math
from functools import partial
import jax
import jax.numpy as jnp
import numpy as np
from jax import lax

MODEL_WIDTH = 1024
H = 16
KVH = 8
HD = 64
FF = 512
E = 32
TOP = 8
SEQ = 1536
TOK_DEV = 192
TOKENS = 24576
NSEQ = 16
HQ = 1024
KEY_VALUE_WIDTH = 512
CAP = 60


def draw_experts(key, part):
    key = jax.random.fold_in(key, 11)
    normal_draw = jnp.clip(jax.random.normal(key, (E, 3, MODEL_WIDTH, FF), jnp.float32), -4.0, 4.0)
    slice_scale = jnp.array([MODEL_WIDTH ** (-0.5), MODEL_WIDTH ** (-0.5), 4.0 * FF ** (-0.5)], jnp.float32)
    return (normal_draw * slice_scale[None, :, None, None]).astype(jnp.bfloat16)


def draw_segments(key, part):
    key = jax.random.fold_in(key, 5)
    front_key, back_key = jax.random.split(key)
    sequence_count = TOKENS // SEQ
    cut_front = jax.random.randint(front_key, (sequence_count,), 1, SEQ // 8)
    cut_back = jax.random.randint(back_key, (sequence_count,), SEQ - SEQ // 8 + 1, SEQ)
    token_place = jnp.arange(SEQ, dtype=jnp.int32)
    document = (token_place[None, :] >= cut_front[:, None]).astype(jnp.int32) + (token_place[None, :] >= cut_back[:, None]).astype(jnp.int32)
    numbers = document + 3 * jnp.arange(sequence_count, dtype=jnp.int32)[:, None]
    return numbers.reshape(TOKENS).astype(jnp.int32)


def levels(rng, extent, cuts, low, top_value):
    gain = 1.0
    for dim, parts in cuts:
        heights = jax.random.uniform(jax.random.fold_in(jax.random.fold_in(rng, 6), dim), (parts,), jnp.float32, low / len(cuts), top_value / len(cuts))
        gain = gain * jnp.repeat(jnp.exp(heights), extent[dim] // parts).reshape((-1,) + (1,) * (len(extent) - 1 - dim))
    return gain


def shared_out(stream_key, own, number, rows, amount, top, most, lean):
    sequence = jax.random.permutation(stream_key, amount)
    crowded, common = portions_of(amount, rows * top, most, lean, True), portions_of(amount, rows * top, most, lean, False)
    places = jnp.arange(amount)

    def named(sizes, rotation):
        used = int((sizes > 0).sum())
        fixed = max(1, used // 4)
        moved = fixed + (places - fixed + rotation * (used - fixed)) % max(1, amount - fixed)
        return jnp.zeros((amount,), jnp.int32).at[sequence[jnp.where(places < fixed, places, moved)]].set(jnp.asarray(sizes, jnp.int32))

    sizes = jnp.where(number % 4 == 0, named(crowded, number // 4), named(common, number - number // 4 - 1))
    mixed = jax.random.permutation(jax.random.fold_in(own, 3), amount)
    giver, sink = mixed[0:amount // 2 * 2:2], mixed[1:amount // 2 * 2:2]
    slack = jnp.minimum(sizes[giver] - 1, most - sizes[sink]) // 2
    slack = jnp.where((giver == sequence[0]) | (sink == sequence[0]) | (sizes[sink] == 0), 0, jnp.maximum(slack, 0))
    moved = jax.random.randint(jax.random.fold_in(own, 4), (amount // 2,), 0, 1 << 20) % (slack + 1)
    sizes = sizes.at[giver].add(-moved).at[sink].add(moved)
    items = jnp.searchsorted(jnp.cumsum(sizes), jnp.arange(rows * top), side="right").astype(jnp.int32)
    grid = items.reshape(top, rows).T
    grid = grid[jax.random.permutation(jax.random.fold_in(own, 1), rows)]
    rotation = jax.random.randint(jax.random.fold_in(own, 2), (rows, 1), 0, top)
    return jnp.take_along_axis(grid, (jnp.arange(top)[None, :] + rotation) % top, axis=1)


def portions_of(count, total, most, slope, full):
    loads = [(1 << 20) // math.isqrt(standing ** slope) + 1 for standing in range(1, count + 1)]
    largest = most if full else min(most, max(-(-total // count), total * loads[0] // sum(loads)))
    least = 1 if total - largest >= count - 1 else 0
    holding, surplus = [largest] + [least] * (count - 1), total - largest - least * (count - 1)
    while surplus > 0:
        movable = [i for i in range(1, count) if holding[i] < largest] or [i for i in range(1, count) if holding[i] < most]
        mass, budget = sum([loads[i] for i in movable]), surplus
        for i in movable:
            addition = min(most - holding[i], max(1, budget * loads[i] // mass), surplus)
            holding[i] = holding[i] + addition
            surplus = surplus - addition
    return np.array(holding)


def gaussian(rng, dims, width, bound, cuts=(), held_as=jnp.bfloat16):
    factor_of = levels(rng, dims, cuts, -0.22, 0.18) if cuts else 1.0
    drawn = jax.random.normal(rng, dims, jnp.float32) * width * factor_of
    return jnp.minimum(jnp.maximum(drawn, -bound), bound).astype(held_as)


def setup_inputs(seed: int = 0) -> dict:
    key_of = jax.random.split(jax.random.key(seed), 13)
    tokens = gaussian(key_of[0], (TOKENS, MODEL_WIDTH), 1.0, 6.0, ((0, 128),))
    norm_one = jnp.clip(1.0 + 0.1 * jax.random.normal(key_of[1], (MODEL_WIDTH,), jnp.float32), 0.5, 1.5).astype(jnp.bfloat16)
    query_weight = gaussian(key_of[2], (MODEL_WIDTH, HQ), MODEL_WIDTH ** -0.5, 0.1875, ((0, 16),))
    key_matrix = gaussian(key_of[3], (MODEL_WIDTH, KEY_VALUE_WIDTH), MODEL_WIDTH ** -0.5, 0.1875, ((0, 16),))
    value_matrix = gaussian(key_of[4], (MODEL_WIDTH, KEY_VALUE_WIDTH), MODEL_WIDTH ** -0.5, 0.1875, ((0, 16),))
    out_weight = gaussian(key_of[5], (HQ, MODEL_WIDTH), (HQ // 64) ** -0.5, 1.5, ((0, 16),))
    norm_two = jnp.clip(1.0 + 0.1 * jax.random.normal(key_of[6], (MODEL_WIDTH,), jnp.float32), 0.5, 1.5).astype(jnp.bfloat16)
    router = gaussian(key_of[7], (MODEL_WIDTH, E), (4 * MODEL_WIDTH) ** -0.5, 0.09375, ((0, 16),))
    experts = draw_experts(jax.random.fold_in(key_of[12], 71), 0)
    routes_keys = jax.random.split(jax.random.fold_in(key_of[9], 1), TOKENS // TOK_DEV)
    routes_turns = jax.random.permutation(jax.random.fold_in(key_of[9], 3), TOKENS // TOK_DEV)
    routes = jax.vmap(lambda own, number: shared_out(jax.random.fold_in(key_of[9], 2), own, number, TOK_DEV, E, TOP, CAP, 1))(routes_keys, routes_turns).reshape((TOKENS, TOP))
    segments = draw_segments(jax.random.fold_in(key_of[12], 71), 0)
    cotangent = gaussian(key_of[11], (TOKENS, MODEL_WIDTH), 1.0, 6.0, ((0, 128),))
    return dict(tokens=tokens, norm_one=norm_one, query_weight=query_weight, key_matrix=key_matrix, value_matrix=value_matrix, out_weight=out_weight, norm_two=norm_two, router=router, experts=experts, routes=routes, segments=segments, cotangent=cotangent)


@jax.custom_vjp
def low(v):
    return lax.optimization_barrier(v.astype(jnp.bfloat16)).astype(jnp.float32)

@jax.custom_vjp
def low_back(v):
    return v

def low_keep(v):
    return (low(v), None)

def low_pass(kept, grad):
    return (grad,)

def back_keep(v):
    return (v, None)

def back_low(kept, grad):
    return (low(grad),)
low.defvjp(low_keep, low_pass)
low_back.defvjp(back_keep, back_low)
EPSILON = 1e-06
HIGHEST = lax.Precision.HIGHEST
MASKED = -1e+30

def rms_norm(value_vectors, gain_vector):
    inverse = lax.rsqrt(lax.optimization_barrier(jnp.mean(value_vectors * value_vectors, axis=-1, keepdims=True)) + EPSILON)
    return value_vectors * inverse * gain_vector

def rotate(value_vectors, positions):
    half_width = value_vectors.shape[-1] // 2
    frequency = 10000.0 ** (-2.0 * jnp.arange(half_width, dtype=jnp.float32) / value_vectors.shape[-1])
    angles = positions[:, None] * frequency[None, :]
    cosine = jnp.cos(angles)[:, None, :]
    sine_part = jnp.sin(angles)[:, None, :]
    front_half = value_vectors[..., :half_width]
    back_half = value_vectors[..., half_width:]
    return jnp.concatenate([front_half * cosine - back_half * sine_part, front_half * sine_part + back_half * cosine], axis=-1)

def attend_sequence(pieces):
    queries, keys, value_vectors, segment_ids = pieces
    scores = jnp.einsum('qhgd,khd->hgqk', queries, keys, precision=HIGHEST) * HD ** (-0.5)
    scores = low_back(scores)
    places = jnp.arange(segment_ids.shape[0])
    allowed = (places[None, :] <= places[:, None]) & (segment_ids[None, :] == segment_ids[:, None])
    chances = low(jax.nn.softmax(jnp.where(allowed, scores, MASKED), axis=-1))
    return jnp.einsum('hgqk,khd->qhgd', chances, value_vectors, precision=HIGHEST)

def expert_block(experts, pieces):
    normed_rows, picks, gate_fraction = pieces
    flat_picks = picks.reshape(-1)
    onehot = (flat_picks[:, None] == jnp.arange(E, dtype=jnp.int32)[None, :]).astype(jnp.int32)
    before = jnp.cumsum(onehot, axis=0) - onehot
    slot_number = lax.optimization_barrier(jnp.sum(before * onehot, axis=1))
    target = (flat_picks * CAP + slot_number).astype(jnp.int32)
    source = jnp.zeros((E * CAP,), jnp.int32).at[target].set(jnp.arange(flat_picks.shape[0], dtype=jnp.int32))
    live_slot = jnp.zeros((E * CAP,), jnp.float32).at[target].set(1.0)
    copies = low_back(jnp.repeat(normed_rows, TOP, axis=0))
    dispatched = (copies[source] * live_slot[:, None]).reshape(E, CAP, MODEL_WIDTH)
    gate_part = low_back(jnp.einsum('ecd,edf->ecf', dispatched, experts[:, 0], precision=HIGHEST))
    up_part = low_back(jnp.einsum('ecd,edf->ecf', dispatched, experts[:, 1], precision=HIGHEST))
    hidden = low(jax.nn.silu(gate_part) * up_part)
    produced = low_back(low(jnp.einsum('ecf,edf->ecd', hidden, experts[:, 2], precision=HIGHEST)))
    picked = produced.reshape(E * CAP, MODEL_WIDTH)[target].reshape(TOK_DEV, TOP, MODEL_WIDTH)
    return lax.optimization_barrier(jnp.sum(picked * gate_fraction[:, :, None], axis=1))

def forward(tokens, norm_one, query_weight, key_matrix, value_matrix, out_weight, norm_two, router, experts, routes, segments):
    group_size = H // KVH
    positions = (jnp.arange(TOKENS) % SEQ).astype(jnp.float32)
    normed = low(rms_norm(tokens, norm_one))
    queries = low(rotate(low_back(jnp.dot(normed, query_weight, precision=HIGHEST)).reshape(TOKENS, H, HD), positions))
    keys = low(rotate(low_back(jnp.dot(normed, key_matrix, precision=HIGHEST)).reshape(TOKENS, KVH, HD), positions))
    value_vectors = low(low_back(jnp.dot(normed, value_matrix, precision=HIGHEST)))
    mixed = lax.map(jax.checkpoint(attend_sequence), (queries.reshape(NSEQ, SEQ, KVH, group_size, HD), keys.reshape(NSEQ, SEQ, KVH, HD), value_vectors.reshape(NSEQ, SEQ, KVH, HD), segments.reshape(NSEQ, SEQ)))
    mixed = low(low_back(mixed.reshape(TOKENS, HQ)))
    middle = tokens + low_back(jnp.dot(mixed, out_weight, precision=HIGHEST))
    normed_two = low(rms_norm(middle, norm_two))
    logits = low_back(jnp.dot(normed_two, router, precision=HIGHEST))
    gate_fraction = jax.nn.softmax(jnp.take_along_axis(logits, routes, axis=1), axis=-1)
    block_count = TOKENS // TOK_DEV
    combined = lax.map(jax.checkpoint(partial(expert_block, experts)), (normed_two.reshape(block_count, TOK_DEV, MODEL_WIDTH), routes.reshape(block_count, TOK_DEV, TOP), gate_fraction.reshape(block_count, TOK_DEV, TOP)))
    return middle + combined.reshape(TOKENS, MODEL_WIDTH)

def reference(tokens, norm_one, query_weight, key_matrix, value_matrix, out_weight, norm_two, router, experts, routes, segments, cotangent):
    floats = tuple((argument.astype(jnp.float32) for argument in (tokens, norm_one, query_weight, key_matrix, value_matrix, out_weight, norm_two, router, experts)))

    def whole_layer(*arrays):
        return forward(*arrays, routes, segments)
    result, reverse_product = jax.vjp(whole_layer, *floats)
    gradients = reverse_product(cotangent.astype(jnp.float32))
    return (result.astype(jnp.bfloat16), gradients[0].astype(jnp.bfloat16), gradients[1], gradients[2], gradients[3], gradients[4], gradients[5], gradients[6], gradients[7], gradients[8])
```

```python
import jax
import jax.numpy as jnp
from jax import lax
from jax.experimental import pallas as pl
from jax.experimental.pallas import tpu as pltpu
from jax.sharding import PartitionSpec as P

D = 1024
H = 16
KVH = 8
HD = 64
FF = 512
E = 32
TOP = 8
SEQ = 1536
TOK = 192
NS = 16
NR = 8
SLOTS = 64
QB = 256
NQ = SEQ // QB
EPSILON = 1e-06
MASKED = -1e30
SCALE = HD ** (-0.5)
BF = jnp.bfloat16
F32 = jnp.float32

NT = (((1,), (1,)), ((), ()))
TN = (((0,), (0,)), ((), ()))


def mm(a, b, dims=(((1,), (0,)), ((), ()))):
    return lax.dot_general(a, b, dims, preferred_element_type=F32)


def split_all(x, axis):
    return lax.all_to_all(x, axis, 0, 0, tiled=True)


def spread_all(x, axis, count):
    return split_all(jnp.broadcast_to(x[None], (count,) + x.shape), axis)


def stacked_heads(block):
    return jnp.concatenate([block[:, :HD], block[:, HD:]], axis=0)


def allowed_keys(key_block, query_block, start_row):
    key_index = lax.broadcasted_iota(jnp.int32, (QB, 2 * QB), 0) + key_block * QB
    column = lax.broadcasted_iota(jnp.int32, (1, 2 * QB), 1)
    query_row = jnp.where(column >= QB, column - QB, column) + query_block * QB
    return (key_index >= start_row) & (key_index <= query_row)


def attend_kernel(q_ref, k_ref, v_ref, start_ref, out_ref, lse_ref):
    i = pl.program_id(0)
    q2 = stacked_heads(q_ref[...])
    start_row = jnp.concatenate([start_ref[0], start_ref[0]], axis=1)

    def step(j, carry):
        largest, summed, total = carry
        rows = pl.ds(pl.multiple_of(j * QB, QB), QB)
        scores = mm(k_ref[rows, :], q2, NT)
        scores = jnp.where(allowed_keys(j, i, start_row), scores, MASKED)
        newest = jnp.maximum(largest, jnp.max(scores, axis=0, keepdims=True))
        chances = jnp.exp(scores - newest)
        factor = jnp.exp(largest - newest)
        summed = summed * factor + jnp.sum(chances, axis=0, keepdims=True)
        total = total * factor + mm(v_ref[rows, :], chances.astype(BF), TN)
        return (newest, summed, total)

    largest, summed, total = lax.fori_loop(
        0,
        i + 1,
        step,
        (
            jnp.full((1, 2 * QB), MASKED, F32),
            jnp.zeros((1, 2 * QB), F32),
            jnp.zeros((HD, 2 * QB), F32),
        ),
    )
    total = total / summed
    out_ref[...] = jnp.concatenate([total[:, :QB], total[:, QB:]], axis=0).T.astype(BF)
    lse_ref[0] = largest + jnp.log(summed)


def attend(q, k, v, start):
    whole = lambda width: pl.BlockSpec((SEQ, width), lambda i: (0, 0))
    return pl.pallas_call(
        attend_kernel,
        grid=(NQ,),
        in_specs=[
            pl.BlockSpec((QB, 2 * HD), lambda i: (i, 0)),
            whole(HD),
            whole(HD),
            pl.BlockSpec((1, 1, QB), lambda i: (i, 0, 0)),
        ],
        out_specs=[
            pl.BlockSpec((QB, 2 * HD), lambda i: (i, 0)),
            pl.BlockSpec((1, 1, 2 * QB), lambda i: (i, 0, 0)),
        ],
        out_shape=[
            jax.ShapeDtypeStruct((SEQ, 2 * HD), BF),
            jax.ShapeDtypeStruct((NQ, 1, 2 * QB), F32),
        ],
        compiler_params=pltpu.CompilerParams(vmem_limit_bytes=40 * 1024 * 1024),
    )(q, k, v, start)


def attend_back_kernel(
    q_ref,
    k_ref,
    v_ref,
    grad_ref,
    start_ref,
    lse_ref,
    cos_t_ref,
    sin_t_ref,
    cos_ref,
    sin_ref,
    dq_ref,
    dkv_ref,
    chances_ref,
    pressure_ref,
    dk_ref,
    dv_ref,
):
    i = pl.program_id(0)

    @pl.when(i == 0)
    def clear():
        dk_ref[...] = jnp.zeros_like(dk_ref)
        dv_ref[...] = jnp.zeros_like(dv_ref)

    q2 = stacked_heads(q_ref[...])
    grad2 = stacked_heads(grad_ref[...])
    start_row = jnp.concatenate([start_ref[0], start_ref[0]], axis=1)
    lse = lse_ref[0]

    def first(j, delta):
        rows = pl.ds(pl.multiple_of(j * QB, QB), QB)
        scores = mm(k_ref[rows, :], q2, NT)
        chances = jnp.where(allowed_keys(j, i, start_row), jnp.exp(scores - lse), 0.0)
        pressure = mm(v_ref[rows, :], grad2, NT)
        chances_ref[rows, :] = chances
        pressure_ref[rows, :] = pressure
        return delta + jnp.sum(chances * pressure, axis=0, keepdims=True)

    delta = lax.fori_loop(0, i + 1, first, jnp.zeros((1, 2 * QB), F32))

    def second(j, total):
        rows = pl.ds(pl.multiple_of(j * QB, QB), QB)
        chances = chances_ref[rows, :]
        score_grad = (chances * (pressure_ref[rows, :] - delta)).astype(BF)
        dv_ref[rows, :] += mm(chances.astype(BF), grad2)
        dk_ref[rows, :] += mm(score_grad, q2)
        return total + mm(k_ref[rows, :], score_grad, TN)

    total = lax.fori_loop(0, i + 1, second, jnp.zeros((HD, 2 * QB), F32)) * SCALE
    cosine, sine = cos_t_ref[...], sin_t_ref[...]
    half = HD // 2
    parts = []
    for head in range(2):
        front = total[:half, head * QB : (head + 1) * QB]
        back = total[half:, head * QB : (head + 1) * QB]
        parts += [front * cosine + back * sine, back * cosine - front * sine]
    dq_ref[...] = jnp.concatenate(parts, axis=0).T.astype(BF)

    @pl.when(i == NQ - 1)
    def finish():
        for j in range(NQ):
            rows = slice(j * QB, (j + 1) * QB)
            dk = dk_ref[rows, :]
            swapped = jnp.concatenate([dk[:, half:], dk[:, :half]], axis=1)
            dk = dk * cos_ref[rows, :] - swapped * sin_ref[rows, :]
            dkv_ref[rows, :] = jnp.concatenate([dk, dv_ref[rows, :]], axis=1).astype(BF)


def attend_back(q, k, v, grad, start, lse, cos_t, sin_t, cos, sin):
    whole = lambda width: pl.BlockSpec((SEQ, width), lambda i: (0, 0))
    block = pl.BlockSpec((QB, 2 * HD), lambda i: (i, 0))
    table = pl.BlockSpec((HD // 2, QB), lambda i: (0, i))
    return pl.pallas_call(
        attend_back_kernel,
        grid=(NQ,),
        in_specs=[
            block,
            whole(HD),
            whole(HD),
            block,
            pl.BlockSpec((1, 1, QB), lambda i: (i, 0, 0)),
            pl.BlockSpec((1, 1, 2 * QB), lambda i: (i, 0, 0)),
            table,
            table,
            whole(HD),
            whole(HD),
        ],
        out_specs=[block, whole(2 * HD)],
        out_shape=[
            jax.ShapeDtypeStruct((SEQ, 2 * HD), BF),
            jax.ShapeDtypeStruct((SEQ, 2 * HD), BF),
        ],
        scratch_shapes=[
            pltpu.VMEM((SEQ, 2 * QB), F32),
            pltpu.VMEM((SEQ, 2 * QB), F32),
            pltpu.VMEM((SEQ, HD), F32),
            pltpu.VMEM((SEQ, HD), F32),
        ],
        compiler_params=pltpu.CompilerParams(vmem_limit_bytes=40 * 1024 * 1024),
    )(q, k, v, grad, start, lse, cos_t, sin_t, cos, sin)


def swap_halves(weights):
    parts = weights.reshape(weights.shape[0], -1, 2, HD // 2)
    return parts[:, :, ::-1, :].reshape(weights.shape)


def hi_lo(value):
    high = value.astype(BF)
    rest = value - high.astype(F32)
    middle = rest.astype(BF)
    return high, middle, (rest - middle.astype(F32)).astype(BF)


def per_device(
    tokens,
    norm_one,
    query_weight,
    key_matrix,
    value_matrix,
    out_weight,
    norm_two,
    router,
    experts,
    routes,
    segments,
    cotangent,
):
    shard = lax.axis_index("shard")
    replica = lax.axis_index("replica")

    segment_row = jnp.pad(segments.astype(BF)[None, :], ((0, 15), (0, D - TOK)))
    sequence = spread_all(jnp.concatenate([tokens, segment_row], axis=0), "replica", NR)
    tokens_seq = sequence[:, :TOK].reshape(SEQ, D)
    segments_seq = sequence[:, TOK, :TOK].astype(jnp.int32).reshape(SEQ)

    own_heads = jnp.concatenate(
        [
            lax.dynamic_slice(query_weight, (0, replica * 128), (64, 128)),
            lax.dynamic_slice(key_matrix, (0, replica * HD), (64, HD)),
            lax.dynamic_slice(value_matrix, (0, replica * HD), (64, HD)),
        ],
        axis=1,
    )
    small = jnp.concatenate(
        [out_weight, own_heads, router, norm_one[:, None], norm_two[:, None], jnp.zeros((64, 94), BF)],
        axis=1,
    )
    gathered = lax.all_gather(small, "shard", axis=0, tiled=True)
    out_full = gathered[:, :1024]
    heads_full = gathered[:, 1024:1280]
    router_full = gathered[:, 1280:1312]
    gain_one = gathered[:, 1312].astype(F32)
    gain_two = gathered[:, 1313].astype(F32)

    chosen = jnp.any(routes[:, :, None] == jnp.arange(E, dtype=jnp.int32), axis=1)
    earlier = jnp.tril(jnp.ones((TOK, TOK), BF), -1)
    slot = jnp.where(chosen, mm(earlier, chosen.astype(BF)), -1.0)
    cot_rows = jnp.concatenate([cotangent, slot.astype(BF), jnp.zeros((TOK, 96), BF)], axis=1)
    cot_all = lax.all_gather(cot_rows, "shard", axis=0, tiled=True)

    half = HD // 2
    frequency = 10000.0 ** (-2.0 * jnp.arange(half, dtype=F32) / HD)
    angles = jnp.arange(SEQ, dtype=F32)[:, None] * frequency[None, :]
    cosine, sine = jnp.cos(angles), jnp.sin(angles)
    cos_head = jnp.concatenate([cosine, cosine], axis=1)
    sin_head = jnp.concatenate([-sine, sine], axis=1)
    wide = tokens_seq.astype(F32)
    inverse = lax.rsqrt(jnp.mean(wide * wide, axis=-1, keepdims=True) + EPSILON)
    normed_one = (wide * inverse * gain_one).astype(BF)
    weights_ext = jnp.concatenate([heads_full, swap_halves(heads_full[:, :192])], axis=1)
    raw = mm(normed_one, weights_ext)
    turned = raw[:, :192] * jnp.tile(cos_head, (1, 3)) + raw[:, 256:448] * jnp.tile(sin_head, (1, 3))
    q_low = (turned[:, :128].astype(BF).astype(F32) * SCALE).astype(BF)
    k_low = turned[:, 128:192].astype(BF)
    v_low = raw[:, 192:256].astype(BF)
    first_segment = shard * 3
    count_one = jnp.sum((segments_seq == first_segment).astype(jnp.int32))
    count_two = jnp.sum((segments_seq == first_segment + 1).astype(jnp.int32))
    start = jnp.where(
        segments_seq == first_segment,
        0,
        jnp.where(segments_seq == first_segment + 1, count_one, count_one + count_two),
    ).reshape(NQ, 1, QB)
    mixed_heads, lse = attend(q_low, k_low, v_low, start)

    mixed = split_all(mixed_heads.reshape(NR, TOK, 128), "replica")
    mixed_low = mixed.transpose(1, 0, 2).reshape(TOK, H * HD)
    tokens_wide = tokens.astype(F32)
    middle = tokens_wide + mm(mixed_low, out_full)
    inverse_two = lax.rsqrt(jnp.mean(middle * middle, axis=-1, keepdims=True) + EPSILON)
    normed_two = (middle * inverse_two * gain_two).astype(BF)
    logits = jnp.where(chosen, mm(normed_two, router_full), MASKED)
    powers = jnp.where(chosen, jnp.exp(logits - jnp.max(logits, axis=-1, keepdims=True)), 0.0)
    gates = powers / jnp.sum(powers, axis=-1, keepdims=True)

    gate_high, gate_middle, gate_low = hi_lo(gates)
    rows_out = jnp.concatenate(
        [normed_two, gate_high, gate_middle, gate_low, jnp.zeros((TOK, 32), BF)], axis=1
    )
    rows_all = lax.all_gather(rows_out, "shard", axis=0, tiled=True)

    def own_columns(array, first):
        picked = lax.dynamic_slice(array, (0, first + 2 * shard), (NS * TOK, 2))
        return picked.astype(F32).reshape(NS, TOK, 2).transpose(0, 2, 1)

    own_slots = own_columns(cot_all, 1024)
    own_gates = own_columns(rows_all, 1024) + own_columns(rows_all, 1056) + own_columns(rows_all, 1088)
    slot_index = jnp.arange(SLOTS, dtype=F32)
    picks = own_slots[:, :, None, :] == slot_index[None, None, :, None]
    picks_low = picks.astype(BF)
    slot_gates = jnp.sum(jnp.where(picks, own_gates[:, :, None, :], 0.0), axis=-1)
    slot_gates = slot_gates.transpose(1, 0, 2).reshape(2, NS * SLOTS, 1)

    def pick_rows(array):
        return (
            jnp.einsum(
                "bect,btd->ebcd",
                picks_low,
                array[:, :D].reshape(NS, TOK, D),
                preferred_element_type=F32,
            )
            .astype(BF)
            .reshape(2, NS * SLOTS, D)
        )

    arrived = pick_rows(rows_all)
    cot_arrived = pick_rows(cot_all)
    gate_w, up_w, down_w = experts[:, 0], experts[:, 1], experts[:, 2]
    bmm = lambda text, a, b: jnp.einsum(text, a, b, preferred_element_type=F32)
    gate_part = bmm("erd,edf->erf", arrived, gate_w)
    up_part = bmm("erd,edf->erf", arrived, up_w)
    sigmoid = jax.nn.sigmoid(gate_part)
    hidden = (gate_part * sigmoid * up_part).astype(BF)
    produced = bmm("erf,edf->erd", hidden, down_w).astype(BF)
    gate_grads = jnp.sum(cot_arrived.astype(F32) * produced.astype(F32), axis=-1)
    grad_out = (slot_gates * cot_arrived.astype(F32)).astype(BF)
    grad_hidden = bmm("erd,edf->erf", grad_out, down_w)
    grad_gate = (grad_hidden * up_part * sigmoid * (1.0 + gate_part * (1.0 - sigmoid))).astype(BF)
    grad_up = (grad_hidden * (gate_part * sigmoid)).astype(BF)
    grad_in = (
        bmm("erf,edf->erd", grad_gate, gate_w) + bmm("erf,edf->erd", grad_up, up_w)
    ).astype(BF)
    expert_grad = jnp.stack(
        [
            bmm("erd,erf->edf", arrived, grad_gate),
            bmm("erd,erf->edf", arrived, grad_up),
            bmm("erd,erf->edf", grad_out, hidden),
        ],
        axis=1,
    ).astype(BF)

    gg = jnp.stack(hi_lo(gate_grads.reshape(2, NS, SLOTS)), axis=2)
    gg = jnp.pad(gg, ((0, 0), (0, 0), (0, 1), (0, D - SLOTS)))
    grad_in = jnp.concatenate([grad_in.reshape(2, NS, SLOTS, D)[:, :, :60], gg], axis=2)
    back = split_all(grad_in.transpose(1, 0, 2, 3), "shard").reshape(E, SLOTS, D)
    returned = split_all(
        produced.reshape(2, NS, SLOTS, D).transpose(1, 0, 2, 3), "shard"
    ).reshape(E * SLOTS, D)
    expert_parts = split_all(expert_grad.reshape(NR, 2 * 3 * D // NR, FF), "replica")
    expert_sum = jnp.sum(expert_parts.reshape(NR, -1, FF).astype(F32), axis=0).astype(BF)
    expert_total = spread_all(expert_sum, "replica", NR).reshape(2, 3, D, FF).astype(F32)

    spots = slot[:, :, None] == slot_index
    spots_low = spots.astype(BF).reshape(TOK, E * SLOTS)
    grad_rows = mm(spots_low, back.reshape(E * SLOTS, D))
    gg_back = jnp.sum(back[:, 60:63, :SLOTS].astype(F32), axis=1)
    gate_grad = jnp.sum(jnp.where(spots, gg_back[None], 0.0), axis=-1)
    chosen_grad = gates * (gate_grad - jnp.sum(gates * gate_grad, axis=-1, keepdims=True))
    logit_grad = chosen_grad.astype(BF)
    weighted_high = jnp.where(spots, gate_high[:, :, None], jnp.zeros((), BF)).reshape(TOK, E * SLOTS)
    weighted_low = jnp.where(spots, gate_middle[:, :, None], jnp.zeros((), BF)).reshape(TOK, E * SLOTS)
    layer_out = (middle + mm(weighted_high, returned) + mm(weighted_low, returned)).astype(BF)

    normed_two_grad = mm(logit_grad, router_full, NT) + grad_rows
    router_grad = mm(normed_two, logit_grad, TN)
    hat = middle * inverse_two
    gain_two_grad = jnp.sum(normed_two_grad * hat, axis=0)
    dyg = normed_two_grad * gain_two
    middle_grad = cotangent.astype(F32) + inverse_two * (
        dyg - hat * jnp.mean(dyg * hat, axis=-1, keepdims=True)
    )
    branch_grad = middle_grad.astype(BF)
    out_grad = mm(mixed_low, branch_grad, TN)
    mixed_grad = mm(branch_grad, out_full, NT).astype(BF)
    grad_heads = split_all(mixed_grad.reshape(TOK, NR, 128).transpose(1, 0, 2), "replica")

    dq, dkv = attend_back(
        q_low,
        k_low,
        v_low,
        grad_heads.reshape(SEQ, 128),
        start,
        lse,
        cosine.T,
        sine.T,
        cos_head,
        sin_head,
    )
    head_grad = jnp.concatenate([dq, dkv], axis=1)
    by_token = split_all(head_grad.reshape(NR, TOK, 256), "replica")
    heads_grad = mm(normed_one, head_grad, TN).astype(BF)
    heads_parts = split_all(heads_grad.reshape(NS, 64, 256), "shard")
    heads_sum = jnp.sum(heads_parts.astype(F32), axis=0).astype(BF)

    dense = jnp.concatenate(
        [out_grad, router_grad, gain_two_grad[:, None], jnp.zeros((D, 95), F32)], axis=1
    ).astype(BF)
    dense_parts = split_all(dense.reshape(NS, 64, 1152), "shard")
    dense_sum = jnp.sum(dense_parts.astype(F32), axis=0).astype(BF)
    dense_here = split_all(dense_sum.reshape(NR, 8, 1152), "replica")
    dense_total = jnp.sum(dense_here.astype(F32), axis=0).astype(BF)

    last = jnp.concatenate([heads_sum.reshape(128, 128), dense_total.reshape(72, 128)], axis=0)
    last = spread_all(jnp.pad(last, ((0, 8), (0, 0))), "replica", NR)
    head_total = last[:, :128].reshape(NR, 64, 256).astype(F32)
    dense_total = last[:, 128:200].reshape(64, 1152).astype(F32)
    query_grad = head_total[:, :, :128].transpose(1, 0, 2).reshape(64, 1024)
    key_grad = head_total[:, :, 128:192].transpose(1, 0, 2).reshape(64, 512)
    value_grad = head_total[:, :, 192:].transpose(1, 0, 2).reshape(64, 512)
    norm_one_grad = (
        jnp.sum(query_grad * query_weight.astype(F32), axis=1)
        + jnp.sum(key_grad * key_matrix.astype(F32), axis=1)
        + jnp.sum(value_grad * value_matrix.astype(F32), axis=1)
    ) / norm_one.astype(F32)

    qkv_full = lax.all_gather(
        jnp.concatenate([query_weight, key_matrix, value_matrix], axis=1), "shard", axis=0, tiled=True
    )
    by_token = by_token.transpose(1, 0, 2)
    normed_grad = (
        mm(by_token[:, :, :128].reshape(TOK, 1024), qkv_full[:, :1024], NT)
        + mm(by_token[:, :, 128:192].reshape(TOK, 512), qkv_full[:, 1024:1536], NT)
        + mm(by_token[:, :, 192:].reshape(TOK, 512), qkv_full[:, 1536:], NT)
    )
    inverse_one = lax.rsqrt(jnp.mean(tokens_wide * tokens_wide, axis=-1, keepdims=True) + EPSILON)
    hat_one = tokens_wide * inverse_one
    dyg_one = normed_grad * gain_one
    tokens_grad = (
        middle_grad
        + inverse_one * (dyg_one - hat_one * jnp.mean(dyg_one * hat_one, axis=-1, keepdims=True))
    ).astype(BF)
    return (
        layer_out,
        tokens_grad,
        norm_one_grad,
        query_grad,
        key_grad,
        value_grad,
        dense_total[:, :1024],
        dense_total[:, 1056],
        dense_total[:, 1024:1056],
        expert_total,
    )


def solution(mesh):
    return jax.shard_map(
        per_device,
        mesh=mesh,
        in_specs=(
            P(("shard", "replica"), None),
            P("shard"),
            P("shard", None),
            P("shard", None),
            P("shard", None),
            P("shard", None),
            P("shard"),
            P("shard", None),
            P("shard", None, None, None),
            P(("shard", "replica"), None),
            P(("shard", "replica")),
            P(("shard", "replica"), None),
        ),
        out_specs=(
            P(("shard", "replica"), None),
            P(("shard", "replica"), None),
            P("shard"),
            P("shard", None),
            P("shard", None),
            P("shard", None),
            P("shard", None),
            P("shard"),
            P("shard", None),
            P("shard", None, None, None),
        ),
        check_vma=False,
    )
```

```python
import jax
import jax.numpy as jnp
from jax import lax
from jax.experimental import pallas as pl
from jax.experimental.pallas import tpu as pltpu
from jax.sharding import PartitionSpec as P

D = 1024
H = 16
KVH = 8
HD = 64
FF = 512
E = 32
TOP = 8
SEQ = 1536
TOK = 192
NS = 16
NR = 8
SLOTS = 64
QB = 256
NQ = SEQ // QB
EPSILON = 1e-06
MASKED = -1e30
SCALE = HD ** (-0.5)
BLOCKS = 4
CHUNKS = NS // BLOCKS
CHUNK_ROWS = BLOCKS * SLOTS
VMEM = 56 * 1024 * 1024
BF = jnp.bfloat16
F32 = jnp.float32

NT = (((1,), (1,)), ((), ()))
TN = (((0,), (0,)), ((), ()))


def mm(a, b, dims=(((1,), (0,)), ((), ()))):
    return lax.dot_general(a, b, dims, preferred_element_type=F32)


def split_all(x, axis):
    return lax.all_to_all(x, axis, 0, 0, tiled=True)


def spread_all(x, axis, count):
    return split_all(jnp.broadcast_to(x[None], (count,) + x.shape), axis)


def stacked_heads(block):
    return jnp.concatenate([block[:, :HD], block[:, HD:]], axis=0)


def allowed_keys(key_block, query_block, start_row):
    key_index = lax.broadcasted_iota(jnp.int32, (QB, 2 * QB), 0) + key_block * QB
    column = lax.broadcasted_iota(jnp.int32, (1, 2 * QB), 1)
    query_row = jnp.where(column >= QB, column - QB, column) + query_block * QB
    return (key_index >= start_row) & (key_index <= query_row)


def rotary_swap(value):
    lane = lax.broadcasted_iota(jnp.int32, value.shape, 1) % HD
    width = value.shape[1]
    return jnp.where(
        lane < HD // 2,
        pltpu.roll(value, width - HD // 2, 1),
        pltpu.roll(value, HD // 2, 1),
    )


def project_kernel(tokens_ref, weight_ref, small_ref, cos_ref, sin_ref, qkv_ref, normed_ref, gains_ref):
    @pl.when(pl.program_id(0) == 0)
    def norm():
        gains = small_ref[...].astype(F32).T[32:40]
        gains_ref[...] = gains
        wide = tokens_ref[...].astype(F32)
        inverse = lax.rsqrt(jnp.mean(wide * wide, axis=-1, keepdims=True) + EPSILON)
        normed_ref[...] = (wide * inverse * gains[0:1]).astype(BF)

    raw = mm(normed_ref[...], weight_ref[...])
    qkv_ref[0] = (raw * cos_ref[...] + rotary_swap(raw) * sin_ref[...]).astype(BF)


def project(tokens, gathered, cos, sin):
    fixed = lambda rows, width, at: pl.BlockSpec((rows, width), lambda g: (0, at))
    return pl.pallas_call(
        project_kernel,
        grid=(NR,),
        in_specs=[
            fixed(TOK, D, 0),
            pl.BlockSpec((D, 256), lambda g: (0, g)),
            fixed(D, 128, 24),
            fixed(TOK, 256, 0),
            fixed(TOK, 256, 0),
        ],
        out_specs=[
            pl.BlockSpec((1, TOK, 256), lambda g: (g, 0, 0)),
            fixed(TOK, D, 0),
            fixed(8, D, 0),
        ],
        out_shape=[
            jax.ShapeDtypeStruct((NR, TOK, 256), BF),
            jax.ShapeDtypeStruct((TOK, D), BF),
            jax.ShapeDtypeStruct((8, D), F32),
        ],
        compiler_params=pltpu.CompilerParams(vmem_limit_bytes=VMEM),
    )(tokens, gathered, gathered, cos, sin)


def attend_kernel(q_ref, kv_ref, start_ref, out_ref, lse_ref):
    i = pl.program_id(0)
    q2 = stacked_heads(q_ref[...])
    start_row = jnp.concatenate([start_ref[0], start_ref[0]], axis=1)

    def step(j, carry):
        largest, summed, total = carry
        kv = kv_ref[pl.ds(pl.multiple_of(j * QB, QB), QB), :]
        scores = mm(kv[:, :HD], q2, NT)
        scores = jnp.where(allowed_keys(j, i, start_row), scores, MASKED)
        newest = jnp.maximum(largest, jnp.max(scores, axis=0, keepdims=True))
        chances = jnp.exp(scores - newest)
        factor = jnp.exp(largest - newest)
        summed = summed * factor + jnp.sum(chances, axis=0, keepdims=True)
        total = total * factor + mm(kv[:, HD:], chances.astype(BF), TN)
        return (newest, summed, total)

    largest, summed, total = lax.fori_loop(
        0,
        i + 1,
        step,
        (
            jnp.full((1, 2 * QB), MASKED, F32),
            jnp.zeros((1, 2 * QB), F32),
            jnp.zeros((HD, 2 * QB), F32),
        ),
    )
    total = total / summed
    out_ref[...] = jnp.concatenate([total[:, :QB], total[:, QB:]], axis=0).T.astype(BF)
    lse_ref[0] = largest + jnp.log(summed)


def attend(qkv, start):
    return pl.pallas_call(
        attend_kernel,
        grid=(NQ,),
        in_specs=[
            pl.BlockSpec((QB, 2 * HD), lambda i: (i, 0)),
            pl.BlockSpec((SEQ, 2 * HD), lambda i: (0, 1)),
            pl.BlockSpec((1, 1, QB), lambda i: (i, 0, 0)),
        ],
        out_specs=[
            pl.BlockSpec((QB, 2 * HD), lambda i: (i, 0)),
            pl.BlockSpec((1, 1, 2 * QB), lambda i: (i, 0, 0)),
        ],
        out_shape=[
            jax.ShapeDtypeStruct((SEQ, 2 * HD), BF),
            jax.ShapeDtypeStruct((NQ, 1, 2 * QB), F32),
        ],
        compiler_params=pltpu.CompilerParams(vmem_limit_bytes=VMEM),
    )(qkv, qkv, start)


def attend_back_kernel(
    q_ref,
    kv_ref,
    grad_ref,
    start_ref,
    lse_ref,
    cos_t_ref,
    sin_t_ref,
    cos_ref,
    sin_ref,
    out_ref,
    chances_ref,
    pressure_ref,
    dk_ref,
    dv_ref,
):
    i = pl.program_id(0)

    @pl.when(i == 0)
    def clear():
        dk_ref[...] = jnp.zeros_like(dk_ref)
        dv_ref[...] = jnp.zeros_like(dv_ref)

    q2 = stacked_heads(q_ref[...])
    grad2 = stacked_heads(grad_ref[...])
    start_row = jnp.concatenate([start_ref[0], start_ref[0]], axis=1)
    lse = lse_ref[0]

    def first(j, delta):
        rows = pl.ds(pl.multiple_of(j * QB, QB), QB)
        kv = kv_ref[rows, :]
        scores = mm(kv[:, :HD], q2, NT)
        chances = jnp.where(allowed_keys(j, i, start_row), jnp.exp(scores - lse), 0.0)
        pressure = mm(kv[:, HD:], grad2, NT)
        chances_ref[rows, :] = chances
        pressure_ref[rows, :] = pressure
        return delta + jnp.sum(chances * pressure, axis=0, keepdims=True)

    delta = lax.fori_loop(0, i + 1, first, jnp.zeros((1, 2 * QB), F32))

    def second(j, total):
        rows = pl.ds(pl.multiple_of(j * QB, QB), QB)
        chances = chances_ref[rows, :]
        score_grad = (chances * (pressure_ref[rows, :] - delta)).astype(BF)
        dv_ref[rows, :] += mm(chances.astype(BF), grad2)
        dk_ref[rows, :] += mm(score_grad, q2)
        return total + mm(kv_ref[rows, :HD], score_grad, TN)

    total = lax.fori_loop(0, i + 1, second, jnp.zeros((HD, 2 * QB), F32)) * SCALE
    cosine, sine = cos_t_ref[...], sin_t_ref[...]
    half = HD // 2
    parts = []
    for head in range(2):
        front = total[:half, head * QB : (head + 1) * QB]
        back = total[half:, head * QB : (head + 1) * QB]
        parts += [front * cosine + back * sine, back * cosine - front * sine]
    query_rows = pl.ds(pl.multiple_of(i * QB, QB), QB)
    out_ref[query_rows, : 2 * HD] = jnp.concatenate(parts, axis=0).T.astype(BF)

    @pl.when(i == NQ - 1)
    def finish():
        for j in range(NQ):
            rows = slice(j * QB, (j + 1) * QB)
            dk = dk_ref[rows, :]
            swapped = jnp.concatenate([dk[:, half:], dk[:, :half]], axis=1)
            dk = dk * cos_ref[rows, :] - swapped * sin_ref[rows, :]
            out_ref[rows, 2 * HD :] = jnp.concatenate([dk, dv_ref[rows, :]], axis=1).astype(BF)


def attend_back(qkv, grad, start, lse, cos_t, sin_t, cos, sin):
    whole = lambda width, at: pl.BlockSpec((SEQ, width), lambda i: (0, at))
    block = pl.BlockSpec((QB, 2 * HD), lambda i: (i, 0))
    table = pl.BlockSpec((HD // 2, QB), lambda i: (0, i))
    return pl.pallas_call(
        attend_back_kernel,
        grid=(NQ,),
        in_specs=[
            block,
            whole(2 * HD, 1),
            block,
            pl.BlockSpec((1, 1, QB), lambda i: (i, 0, 0)),
            pl.BlockSpec((1, 1, 2 * QB), lambda i: (i, 0, 0)),
            table,
            table,
            whole(HD, 0),
            whole(HD, 0),
        ],
        out_specs=whole(4 * HD, 0),
        out_shape=jax.ShapeDtypeStruct((SEQ, 4 * HD), BF),
        scratch_shapes=[
            pltpu.VMEM((SEQ, 2 * QB), F32),
            pltpu.VMEM((SEQ, 2 * QB), F32),
            pltpu.VMEM((SEQ, HD), F32),
            pltpu.VMEM((SEQ, HD), F32),
        ],
        compiler_params=pltpu.CompilerParams(vmem_limit_bytes=VMEM),
    )(qkv, qkv, grad, start, lse, cos_t, sin_t, cos, sin)


def hi_lo(value):
    high = value.astype(BF).astype(F32)
    rest = value - high
    middle = rest.astype(BF).astype(F32)
    return high, middle, (rest - middle).astype(BF).astype(F32)


def route_kernel(
    mixed_ref, tokens_ref, out_ref, small_ref, gains_ref, chosen_ref, middle_ref, rows_ref, gates_ref
):
    mixed = jnp.concatenate([mixed_ref[g] for g in range(NR)], axis=1)
    middle = tokens_ref[...].astype(F32) + mm(mixed, out_ref[...])
    middle_ref[...] = middle
    inverse = lax.rsqrt(jnp.mean(middle * middle, axis=-1, keepdims=True) + EPSILON)
    normed = (middle * inverse * gains_ref[1:2, :]).astype(BF)
    rows_ref[:, :D] = normed
    chosen = chosen_ref[...] > 0.0
    logits = jnp.where(chosen, mm(normed, small_ref[...]), MASKED)
    powers = jnp.exp(logits - jnp.max(logits, axis=-1, keepdims=True))
    powers = jnp.where(chosen, powers, 0.0)
    gates = powers / jnp.sum(powers, axis=-1, keepdims=True)
    gates_ref[...] = gates
    high, middle_part, low = hi_lo(gates)
    rows_ref[:, D:] = (high + pltpu.roll(middle_part, 32, 1) + pltpu.roll(low, 64, 1)).astype(BF)


def route(mixed, tokens, gathered, gains, chosen):
    fixed = lambda rows, width, at: pl.BlockSpec((rows, width), lambda i: (0, at))
    return pl.pallas_call(
        route_kernel,
        grid=(1,),
        in_specs=[
            pl.BlockSpec((NR, TOK, 128), lambda i: (0, 0, 0)),
            fixed(TOK, D, 0),
            fixed(D, D, 2),
            fixed(D, 128, 24),
            fixed(8, D, 0),
            fixed(TOK, 128, 0),
        ],
        out_specs=[fixed(TOK, D, 0), fixed(TOK, D + 128, 0), fixed(TOK, 128, 0)],
        out_shape=[
            jax.ShapeDtypeStruct((TOK, D), F32),
            jax.ShapeDtypeStruct((TOK, D + 128), BF),
            jax.ShapeDtypeStruct((TOK, 128), F32),
        ],
        compiler_params=pltpu.CompilerParams(vmem_limit_bytes=VMEM),
    )(mixed, tokens, gathered, gathered, gains, chosen)


def expert_kernel(
    rows_ref,
    cot_ref,
    slots_ref,
    own_ref,
    weight_ref,
    combined_ref,
    back_ref,
    grad_ref,
    x_ref,
    g_ref,
    hidden_ref,
    dgate_ref,
    dup_ref,
):
    step = pl.program_id(0)

    @pl.when(step < CHUNKS)
    def forward_backward():
        row_index = lax.broadcasted_iota(jnp.int32, (SLOTS, 128), 0)
        lane_index = lax.broadcasted_iota(jnp.int32, (SLOTS, 128), 1)
        slot_index = lax.broadcasted_iota(jnp.int32, (SLOTS, TOK), 0).astype(F32)
        x_parts, cot_parts, all_picks, weighted = [[], []], [[], []], [], []
        for b in range(BLOCKS):
            tokens = slice(b * TOK, (b + 1) * TOK)
            picks = jnp.concatenate(
                [(slots_ref[e, 0, b : b + 1, :] == slot_index).astype(F32) for e in range(2)], axis=0
            ).astype(BF)
            all_picks.append(picks)
            picked = mm(picks, rows_ref[tokens, :])
            picked_cot = mm(picks, cot_ref[tokens, :D])
            for e in range(2):
                x_parts[e].append(picked[e * SLOTS : (e + 1) * SLOTS])
                cot_parts[e].append(picked_cot[e * SLOTS : (e + 1) * SLOTS])
        here = pl.ds(pl.multiple_of(step * CHUNK_ROWS, CHUNK_ROWS), CHUNK_ROWS)
        for e in range(2):
            both = jnp.concatenate(x_parts[e], axis=0)
            gates = jnp.sum(both[:, D:] * own_ref[e], axis=1, keepdims=True)
            x = both[:, :D].astype(BF)
            cot = jnp.concatenate(cot_parts[e], axis=0)
            gate_w, up_w, down_w = weight_ref[e, 0], weight_ref[e, 1], weight_ref[e, 2]
            gate = mm(x, gate_w)
            up = mm(x, up_w)
            sigmoid = 1.0 / (1.0 + jnp.exp(-gate))
            silu = gate * sigmoid
            hidden = (silu * up).astype(BF)
            grad_out = (gates * cot).astype(BF)
            grad_hidden = mm(grad_out, down_w)
            grad_gate = (grad_hidden * up * sigmoid * (1.0 + gate * (1.0 - sigmoid))).astype(BF)
            grad_up = (grad_hidden * silu).astype(BF)
            x_ref[e, here, :] = x
            g_ref[e, here, :] = grad_out
            hidden_ref[e, here, :] = hidden
            dgate_ref[e, here, :] = grad_gate
            dup_ref[e, here, :] = grad_up
            produced = mm(hidden, down_w, NT).astype(BF).astype(F32)
            weighted.append((gates * produced).astype(BF))
            gate_grads = jnp.sum(cot * produced, axis=1, keepdims=True)
            grad_in = mm(grad_gate, gate_w, NT) + mm(grad_up, up_w, NT)
            for b in range(BLOCKS):
                block = slice(b * SLOTS, (b + 1) * SLOTS)
                row = jnp.sum(
                    jnp.where(row_index == lane_index, gate_grads[block], 0.0), axis=0, keepdims=True
                )
                spare = jnp.zeros((SLOTS, 128), F32)
                for place, part in enumerate(hi_lo(row)):
                    spare = jnp.where(row_index == 60 + place, part, spare)
                back_ref[b, e, :, :128] = (grad_in[block, :128] + spare).astype(BF)
                back_ref[b, e, :, 128:] = grad_in[block, 128:].astype(BF)
        for b in range(BLOCKS):
            block = slice(b * SLOTS, (b + 1) * SLOTS)
            rows = jnp.concatenate([weighted[0][block], weighted[1][block]], axis=0)
            combined_ref[b % 2, 0, b // 2] = mm(all_picks[b], rows, TN).astype(BF)

    for e in range(2):
        for n, (left, right) in enumerate(((x_ref, dgate_ref), (x_ref, dup_ref), (g_ref, hidden_ref))):

            @pl.when(step == CHUNKS + 3 * e + n)
            def weight_grads(left=left, right=right, e=e):
                grad_ref[0, 0] = mm(left[e], right[e], TN).astype(BF)


def run_experts(rows, cot, slots, own, experts):
    chunk = lambda i: jnp.minimum(i, CHUNKS - 1)
    after = lambda i: jnp.maximum(i - CHUNKS, 0)
    taken = pl.BlockSpec((BLOCKS * TOK, D + 128), lambda i: (chunk(i), 0))
    made = pl.BlockSpec((BLOCKS, 2, SLOTS, D), lambda i: (chunk(i), 0, 0, 0))
    return pl.pallas_call(
        expert_kernel,
        grid=(CHUNKS + 6,),
        in_specs=[
            taken,
            taken,
            pl.BlockSpec((2, 1, BLOCKS, TOK), lambda i: (0, chunk(i), 0, 0)),
            pl.BlockSpec((2, 1, 128), lambda i: (0, 0, 0)),
            pl.BlockSpec((2, 3, D, FF), lambda i: (0, 0, 0, 0), pipeline_mode=pl.Buffered(1)),
        ],
        out_specs=[
            pl.BlockSpec((2, 1, 2, TOK, D), lambda i: (0, chunk(i), 0, 0, 0)),
            made,
            pl.BlockSpec((1, 1, D, FF), lambda i: (after(i) // 3, after(i) % 3, 0, 0)),
        ],
        out_shape=[
            jax.ShapeDtypeStruct((2, 4, 2, TOK, D), BF),
            jax.ShapeDtypeStruct((NS, 2, SLOTS, D), BF),
            jax.ShapeDtypeStruct((2, 3, D, FF), BF),
        ],
        scratch_shapes=[
            pltpu.VMEM((2, NS * SLOTS, D), BF),
            pltpu.VMEM((2, NS * SLOTS, D), BF),
            pltpu.VMEM((2, NS * SLOTS, FF), BF),
            pltpu.VMEM((2, NS * SLOTS, FF), BF),
            pltpu.VMEM((2, NS * SLOTS, FF), BF),
        ],
        compiler_params=pltpu.CompilerParams(vmem_limit_bytes=VMEM),
    )(rows, cot, slots, own, experts)


def token_kernel(
    back_ref,
    spots_ref,
    spread_ref,
    gate_rows_ref,
    gates_ref,
    cot_ref,
    middle_ref,
    normed_ref,
    gains_ref,
    small_ref,
    out_ref,
    mixed_ref,
    middle_grad_ref,
    mixed_grad_ref,
    dense_ref,
):
    spots = spots_ref[...]
    rows = mm(spots, back_ref[...])
    gate_grad = jnp.zeros((TOK, 128), F32)
    for p in range(3):
        gate_grad += mm(spots * gate_rows_ref[p : p + 1, :], spread_ref[...])
    gates = gates_ref[...]
    chosen_grad = gates * (gate_grad - jnp.sum(gates * gate_grad, axis=-1, keepdims=True))
    logit_grad = chosen_grad.astype(BF)
    normed_grad = mm(logit_grad, small_ref[...], NT) + rows
    middle = middle_ref[...]
    inverse = lax.rsqrt(jnp.mean(middle * middle, axis=-1, keepdims=True) + EPSILON)
    hat = middle * inverse
    scaled = normed_grad * gains_ref[1:2, :]
    middle_grad = cot_ref[...].astype(F32) + inverse * (
        scaled - hat * jnp.mean(scaled * hat, axis=-1, keepdims=True)
    )
    middle_grad_ref[...] = middle_grad
    branch = middle_grad.astype(BF)
    mixed_grad = mm(branch, out_ref[...], NT).astype(BF)
    for g in range(NR):
        mixed_grad_ref[g] = mixed_grad[:, g * 128 : (g + 1) * 128]
    gain_grad = jnp.sum(normed_grad * hat, axis=0, keepdims=True)
    lane = lax.broadcasted_iota(jnp.int32, (D, 128), 1)
    gain_column = jnp.broadcast_to(gain_grad, (128, D)).T
    router_grad = mm(normed_ref[...], logit_grad, TN)
    dense_ref[:, D:] = jnp.where(lane == 32, gain_column, router_grad).astype(BF)
    for g in range(NR):
        dense_ref[g * 128 : (g + 1) * 128, :D] = mm(mixed_ref[g], branch, TN).astype(BF)


def token_back(back, spots, spread, gate_rows, gates, cot, middle, rows, gains, gathered, mixed):
    fixed = lambda count, width, at=0: pl.BlockSpec((count, width), lambda i: (0, at))
    return pl.pallas_call(
        token_kernel,
        grid=(1,),
        in_specs=[
            fixed(E * SLOTS, D),
            fixed(TOK, E * SLOTS),
            fixed(E * SLOTS, 128),
            fixed(3, E * SLOTS),
            fixed(TOK, 128),
            fixed(TOK, D),
            fixed(TOK, D),
            fixed(TOK, D),
            fixed(8, D),
            fixed(D, 128, 24),
            fixed(D, D, 2),
            pl.BlockSpec((NR, TOK, 128), lambda i: (0, 0, 0)),
        ],
        out_specs=[
            fixed(TOK, D),
            pl.BlockSpec((NR, TOK, 128), lambda i: (0, 0, 0)),
            fixed(D, D + 128),
        ],
        out_shape=[
            jax.ShapeDtypeStruct((TOK, D), F32),
            jax.ShapeDtypeStruct((NR, TOK, 128), BF),
            jax.ShapeDtypeStruct((D, D + 128), BF),
        ],
        compiler_params=pltpu.CompilerParams(vmem_limit_bytes=VMEM),
    )(back, spots, spread, gate_rows, gates, cot, middle, rows, gains, gathered, gathered, mixed)


def after(value, *others):
    return lax.optimization_barrier((value,) + others)[0]


def heads_kernel(parts_ref, query_ref, key_ref, value_ref, gain_ref, dq_ref, dk_ref, dv_ref, norm_ref):
    total = jnp.zeros((64, 128), F32)
    for pair in range(NR // 2):
        first, second = parts_ref[2 * pair].astype(F32), parts_ref[2 * pair + 1].astype(F32)
        lanes = slice(pair * 128, (pair + 1) * 128)
        for at, part in ((2 * pair, first), (2 * pair + 1, second)):
            wide = slice(at * 128, (at + 1) * 128)
            dq_ref[:, wide] = part[:, :128]
            total += part[:, :128] * query_ref[:, wide].astype(F32)
        dk = jnp.concatenate([first[:, 128:192], second[:, 128:192]], axis=1)
        dv = jnp.concatenate([first[:, 192:], second[:, 192:]], axis=1)
        dk_ref[:, lanes] = dk
        dv_ref[:, lanes] = dv
        total += dk * key_ref[:, lanes].astype(F32) + dv * value_ref[:, lanes].astype(F32)
    norm_ref[...] = jnp.sum(total, axis=1, keepdims=True) / gain_ref[...]


def finish_heads(parts, query_weight, key_matrix, value_matrix, norm_one):
    return pl.pallas_call(
        heads_kernel,
        out_shape=[
            jax.ShapeDtypeStruct((64, 1024), F32),
            jax.ShapeDtypeStruct((64, 512), F32),
            jax.ShapeDtypeStruct((64, 512), F32),
            jax.ShapeDtypeStruct((64, 1), F32),
        ],
    )(parts, query_weight, key_matrix, value_matrix, norm_one.astype(F32)[:, None])


def widen_kernel(place_ref, rows_ref, *refs):
    refs[-1][...] = rows_ref[...].astype(F32)


def widen(rows, place, total=None):
    block = 512
    steps = rows.shape[0] // block
    given = () if total is None else (total,)
    return pl.pallas_call(
        widen_kernel,
        grid_spec=pltpu.PrefetchScalarGridSpec(
            num_scalar_prefetch=1,
            grid=(steps,),
            in_specs=[pl.BlockSpec((block, FF), lambda i, place: (i, 0))]
            + [pl.BlockSpec(memory_space=pl.ANY)] * len(given),
            out_specs=pl.BlockSpec((block, FF), lambda i, place: (place[0] * steps + i, 0)),
        ),
        out_shape=jax.ShapeDtypeStruct((6 * D, FF), F32),
        input_output_aliases={2: 0} if given else {},
    )(jnp.reshape(place, (1,)).astype(jnp.int32), rows, *given)


def exchange(x, bits, axis="replica"):
    return lax.ppermute(x, axis, [(i, i ^ bits) for i in range(lax.axis_size(axis))])


def halves(x, bit):
    half = x.shape[0] // 2
    take = lambda at: lax.dynamic_slice_in_dim(x, at * half, half, 0)
    return take(bit), take(1 - bit)


def in_order(own, other, bit):
    first = jnp.where(bit == 0, own, other)
    return jnp.concatenate([first, jnp.where(bit == 0, other, own)], axis=0)


def add_low(a, b):
    return (a.astype(F32) + b.astype(F32)).astype(BF)


def per_device(
    tokens,
    norm_one,
    query_weight,
    key_matrix,
    value_matrix,
    out_weight,
    norm_two,
    router,
    experts,
    routes,
    segments,
    cotangent,
):
    shard = lax.axis_index("shard")
    replica = lax.axis_index("replica")
    along_x = replica // 2
    side = replica % 2
    low_bit, high_bit = along_x % 2, along_x // 2
    mixed_bit = low_bit ^ high_bit

    grouped = jnp.concatenate(
        [
            query_weight.reshape(64, NR, 128),
            key_matrix.reshape(64, NR, HD),
            value_matrix.reshape(64, NR, HD),
        ],
        axis=2,
    ).reshape(64, 2048)
    small = jnp.concatenate(
        [router, norm_one[:, None], norm_two[:, None], jnp.zeros((64, 94), BF)], axis=1
    )
    gathered = lax.all_gather(
        jnp.concatenate([grouped, out_weight, small], axis=1), "shard", axis=0, tiled=True
    )

    segments_seq = spread_all(segments, "replica", NR).reshape(SEQ)
    first_segment = shard * 3
    count_one = jnp.sum((segments_seq == first_segment).astype(jnp.int32))
    count_two = jnp.sum((segments_seq == first_segment + 1).astype(jnp.int32))
    start = jnp.where(
        segments_seq == first_segment,
        0,
        jnp.where(segments_seq == first_segment + 1, count_one, count_one + count_two),
    ).reshape(NQ, 1, QB)

    chosen = jnp.any(routes[:, :, None] == jnp.arange(128, dtype=jnp.int32), axis=1)
    earlier = jnp.tril(jnp.ones((TOK, TOK), BF), -1)
    slot = jnp.where(chosen, mm(earlier, chosen.astype(BF)), -1.0)
    cot_rows = jnp.concatenate([cotangent, slot.astype(BF)], axis=1)
    cot_all = lax.all_gather(cot_rows, "shard", axis=0, tiled=True)
    spots = slot[:, :E, None] == jnp.arange(SLOTS, dtype=F32)
    spots = spots.astype(BF).reshape(TOK, E * SLOTS)
    spread = (
        jnp.arange(E * SLOTS)[:, None] // SLOTS == jnp.arange(128)[None, :]
    ).astype(BF)

    half = HD // 2
    frequency = 10000.0 ** (-2.0 * jnp.arange(half, dtype=F32) / HD)
    angles = jnp.arange(SEQ, dtype=F32)[:, None] * frequency[None, :]
    cosine, sine = jnp.cos(angles), jnp.sin(angles)
    cos_head = jnp.concatenate([cosine, cosine], axis=1)
    sin_head = jnp.concatenate([-sine, sine], axis=1)
    cos_here = lax.dynamic_slice(cos_head, (replica * TOK, 0), (TOK, HD))
    sin_here = lax.dynamic_slice(sin_head, (replica * TOK, 0), (TOK, HD))
    cos_group = jnp.concatenate(
        [cos_here * SCALE, cos_here * SCALE, cos_here, jnp.ones((TOK, HD), F32)], axis=1
    )
    sin_group = jnp.concatenate(
        [sin_here * SCALE, sin_here * SCALE, sin_here, jnp.zeros((TOK, HD), F32)], axis=1
    )

    tokens_in, start, spots, spread = lax.optimization_barrier((tokens, start, spots, spread))
    qkv_here, normed_one, gains = project(tokens_in, gathered, cos_group, sin_group)
    qkv = split_all(qkv_here, "replica").reshape(SEQ, 256)
    normed_one, qkv = lax.optimization_barrier((normed_one, qkv))
    normed_pair = in_order(normed_one, exchange(normed_one, 1), side)
    mixed_heads, lse = attend(qkv, start)
    mixed = split_all(mixed_heads.reshape(NR, TOK, 128), "replica")
    mixed, normed_pair = lax.optimization_barrier((mixed, normed_pair))
    normed_pairs = [normed_pair] + [exchange(normed_pair, 2 * k) for k in (1, 2, 3)]
    middle, rows_out, gates = route(mixed, tokens, gathered, gains, chosen.astype(F32))

    rows_all = lax.all_gather(rows_out, "shard", axis=0, tiled=True)
    normed_seq = jnp.concatenate(normed_pairs, axis=0)
    own_slots = lax.dynamic_slice(cot_all, (0, D + 2 * shard), (NS * TOK, 2)).astype(F32)
    own_slots = own_slots.T.reshape(2, CHUNKS, BLOCKS, TOK)
    lane = jnp.arange(128)[None, :]
    own = jnp.stack(
        [((lane % E == 2 * shard + e) & (lane < 3 * E)).astype(F32) for e in range(2)]
    )
    combined, grad_in, expert_grad = run_experts(rows_all, cot_all, own_slots, own, experts)
    back = split_all(after(grad_in, normed_seq), "shard")

    rows = expert_grad.reshape(2, 3 * D, FF)
    keep_a, send_a = halves(rows[0], mixed_bit)
    keep_b, send_b = halves(rows[1], high_bit)
    got_a, got_b = exchange(send_a, 2), exchange(send_b, 6)
    keep_a, send_a = halves(add_low(keep_a, got_a), low_bit)
    keep_b, send_b = halves(add_low(keep_b, got_b), low_bit)
    core, row, layer = shard % 2, shard // 2 % 2, shard // 4
    pick = lambda x, at: lax.dynamic_index_in_dim(x, at, 0, keepdims=False)
    from_core = exchange(pick(combined, 1 - core), 1, "shard")
    back, send_a, send_b, from_core = lax.optimization_barrier((back, send_a, send_b, from_core))
    got_a, got_b = exchange(send_a, 6), exchange(send_b, 2)
    sums = add_low(pick(combined, core), from_core)
    keep = [[pick(sums[:, y], layer), pick(sums[:, y], layer ^ step)] for y, step in ((0, 3), (1, 1))]
    send = [
        jnp.stack([pick(sums[:, y], layer ^ first), pick(sums[:, y], layer ^ 2)])
        for y, first in ((0, 1), (1, 3))
    ]
    layers = [exchange(send[0], 4, "shard"), exchange(send[1], 12, "shard")]

    gate_rows = back.reshape(E, SLOTS, D)[:, 60:63, :SLOTS].transpose(1, 0, 2).reshape(3, E * SLOTS)
    middle_grad, mixed_grad, dense = token_back(
        back.reshape(E * SLOTS, D),
        spots,
        spread,
        gate_rows,
        gates,
        cotangent,
        middle,
        rows_out,
        gains,
        gathered,
        mixed,
    )
    grad_heads = split_all(mixed_grad, "replica").reshape(SEQ, 128)
    grad_heads, got_a, got_b, *layers = lax.optimization_barrier((grad_heads, got_a, got_b, *layers))
    keep = [[add_low(keep[y][n], layers[y][n]) for n in range(2)] for y in range(2)]
    layers = [exchange(keep[0][1], 12, "shard"), exchange(keep[1][1], 4, "shard")]
    keep_a, send_a = halves(add_low(keep_a, got_a), side)
    keep_b, send_b = halves(add_low(keep_b, got_b), side)
    got = exchange(jnp.concatenate([send_a, send_b], axis=0), 1)
    head_grad = attend_back(
        qkv, grad_heads, start, lse, cosine.T, sine.T, cos_head, sin_head
    )
    head_grad, got, *layers = lax.optimization_barrier((head_grad, got, *layers))
    sides = [add_low(keep[y][0], layers[y]) for y in range(2)]
    own_side = jnp.where(row == 0, sides[0], sides[1])
    from_side = exchange(jnp.where(row == 0, sides[1], sides[0]), 2, "shard")
    own = add_low(jnp.concatenate([keep_a, keep_b], axis=0), got)
    other = exchange(own, 1)
    half = own.shape[0] // 2
    head_rows = jnp.concatenate(
        [
            lax.dynamic_slice_in_dim(head_grad, (along_x ^ k) * 2 * TOK, 2 * TOK, 0)
            for k in range(4)
        ],
        axis=0,
    )
    heads_grad = mm(normed_seq, head_rows, TN).astype(BF)
    dense_parts = split_all(after(dense, grad_heads).reshape(NS * NR, 8, 1152), ("shard", "replica"))
    dense_sum = jnp.sum(dense_parts.reshape(NS * NR, 8, 1152).astype(F32), axis=0).astype(BF)
    heads_grad = after(heads_grad, dense_parts)
    heads_parts = split_all(heads_grad.reshape(NS, 64, 256), "shard")
    heads_sum = jnp.sum(heads_parts.astype(F32), axis=0).astype(BF)
    head_grad, heads_parts, other = lax.optimization_barrier((head_grad, heads_parts, other))
    own_a, own_b = in_order(own[:half], other[:half], side), in_order(own[half:], other[half:], side)
    other_a, other_b = exchange(own_a, 6), exchange(own_b, 2)

    by_token = split_all(head_grad.reshape(NR, TOK, 256), "replica")
    normed_grad = mm(by_token.transpose(1, 0, 2).reshape(TOK, 2048), gathered[:, :2048], NT)
    tokens_wide = tokens.astype(F32)
    inverse = lax.rsqrt(jnp.mean(tokens_wide * tokens_wide, axis=-1, keepdims=True) + EPSILON)
    hat = tokens_wide * inverse
    scaled = normed_grad * gains[0:1]
    tokens_grad = (
        middle_grad + inverse * (scaled - hat * jnp.mean(scaled * hat, axis=-1, keepdims=True))
    ).astype(BF)

    layer_out = (middle + own_side.astype(F32) + from_side.astype(F32)).astype(BF)

    last = jnp.concatenate([heads_sum.reshape(128, 128), dense_sum.reshape(72, 128)], axis=0)
    last = jnp.pad(last, ((0, 8), (0, 0)))
    last, by_token, other_a, other_b = lax.optimization_barrier((last, by_token, other_a, other_b))
    own_a, own_b = in_order(own_a, other_a, low_bit), in_order(own_b, other_b, low_bit)
    other_a, other_b = exchange(own_a, 2), exchange(own_b, 6)
    last = spread_all(last, "replica", NR)
    query_grad, key_grad, value_grad, norm_one_grad = finish_heads(
        last[:, :128].reshape(NR, 64, 256), query_weight, key_matrix, value_matrix, norm_one
    )
    dense_last = last[:, 128:200].reshape(64, 1152).astype(F32)
    expert_total = widen(own_a, mixed_bit)
    expert_total = widen(own_b, 2 + high_bit, expert_total)
    expert_total = widen(other_a, 1 - mixed_bit, expert_total)
    expert_total = widen(other_b, 3 - high_bit, expert_total).reshape(2, 3, D, FF)
    return (
        layer_out,
        tokens_grad,
        norm_one_grad[:, 0],
        query_grad,
        key_grad,
        value_grad,
        dense_last[:, :1024],
        dense_last[:, 1056],
        dense_last[:, 1024:1056],
        expert_total,
    )


def solution(mesh):
    return jax.shard_map(
        per_device,
        mesh=mesh,
        in_specs=(
            P(("shard", "replica"), None),
            P("shard"),
            P("shard", None),
            P("shard", None),
            P("shard", None),
            P("shard", None),
            P("shard"),
            P("shard", None),
            P("shard", None, None, None),
            P(("shard", "replica"), None),
            P(("shard", "replica")),
            P(("shard", "replica"), None),
        ),
        out_specs=(
            P(("shard", "replica"), None),
            P(("shard", "replica"), None),
            P("shard"),
            P("shard", None),
            P("shard", None),
            P("shard", None),
            P("shard", None),
            P("shard"),
            P("shard", None),
            P("shard", None, None, None),
        ),
        check_vma=False,
    )
```

```python
import jax
import jax.numpy as jnp
from jax import lax
from jax.experimental import pallas as pl
from jax.experimental.pallas import tpu as pltpu
from jax.sharding import PartitionSpec as P

D = 1024
H = 16
KVH = 8
HD = 64
FF = 512
E = 32
TOP = 8
SEQ = 1536
TOK = 192
NS = 16
NR = 8
SLOTS = 64
QB = 256
NQ = SEQ // QB
EPSILON = 1e-06
MASKED = -1e30
SCALE = HD ** (-0.5)
BLOCKS = 4
CHUNKS = NS // BLOCKS
CHUNK_ROWS = BLOCKS * SLOTS
VMEM = 56 * 1024 * 1024
BF = jnp.bfloat16
F32 = jnp.float32

NT = (((1,), (1,)), ((), ()))
TN = (((0,), (0,)), ((), ()))


def mm(a, b, dims=(((1,), (0,)), ((), ()))):
    return lax.dot_general(a, b, dims, preferred_element_type=F32)


def split_all(x, axis):
    return lax.all_to_all(x, axis, 0, 0, tiled=True)


def spread_all(x, axis, count):
    return split_all(jnp.broadcast_to(x[None], (count,) + x.shape), axis)


def stacked_heads(block):
    return jnp.concatenate([block[:, :HD], block[:, HD:]], axis=0)


def allowed_keys(key_block, query_block, start_row):
    key_index = lax.broadcasted_iota(jnp.int32, (QB, 2 * QB), 0) + key_block * QB
    column = lax.broadcasted_iota(jnp.int32, (1, 2 * QB), 1)
    query_row = jnp.where(column >= QB, column - QB, column) + query_block * QB
    return (key_index >= start_row) & (key_index <= query_row)


def rotary_swap(value):
    lane = lax.broadcasted_iota(jnp.int32, value.shape, 1) % HD
    width = value.shape[1]
    return jnp.where(
        lane < HD // 2,
        pltpu.roll(value, width - HD // 2, 1),
        pltpu.roll(value, HD // 2, 1),
    )


def project_kernel(tokens_ref, weight_ref, small_ref, cos_ref, sin_ref, qkv_ref, normed_ref, gains_ref):
    @pl.when(pl.program_id(0) == 0)
    def norm():
        gains = small_ref[...].astype(F32).T[32:40]
        gains_ref[...] = gains
        wide = tokens_ref[...].astype(F32)
        inverse = lax.rsqrt(jnp.mean(wide * wide, axis=-1, keepdims=True) + EPSILON)
        normed_ref[...] = (wide * inverse * gains[0:1]).astype(BF)

    raw = mm(normed_ref[...], weight_ref[...])
    qkv_ref[0] = (raw * cos_ref[...] + rotary_swap(raw) * sin_ref[...]).astype(BF)


def project(tokens, gathered, cos, sin):
    fixed = lambda rows, width, at: pl.BlockSpec((rows, width), lambda g: (0, at))
    return pl.pallas_call(
        project_kernel,
        grid=(NR,),
        in_specs=[
            fixed(TOK, D, 0),
            pl.BlockSpec((D, 256), lambda g: (0, g)),
            fixed(D, 128, 24),
            fixed(TOK, 256, 0),
            fixed(TOK, 256, 0),
        ],
        out_specs=[
            pl.BlockSpec((1, TOK, 256), lambda g: (g, 0, 0)),
            fixed(TOK, D, 0),
            fixed(8, D, 0),
        ],
        out_shape=[
            jax.ShapeDtypeStruct((NR, TOK, 256), BF),
            jax.ShapeDtypeStruct((TOK, D), BF),
            jax.ShapeDtypeStruct((8, D), F32),
        ],
        compiler_params=pltpu.CompilerParams(vmem_limit_bytes=VMEM),
    )(tokens, gathered, gathered, cos, sin)


def attend_kernel(q_ref, kv_ref, start_ref, out_ref, lse_ref):
    i = pl.program_id(0)
    q2 = stacked_heads(q_ref[...])
    start_row = jnp.concatenate([start_ref[0], start_ref[0]], axis=1)

    def step(j, carry):
        largest, summed, total = carry
        kv = kv_ref[pl.ds(pl.multiple_of(j * QB, QB), QB), :]
        scores = mm(kv[:, :HD], q2, NT)
        scores = jnp.where(allowed_keys(j, i, start_row), scores, MASKED)
        newest = jnp.maximum(largest, jnp.max(scores, axis=0, keepdims=True))
        chances = jnp.exp(scores - newest)
        factor = jnp.exp(largest - newest)
        summed = summed * factor + jnp.sum(chances, axis=0, keepdims=True)
        total = total * factor + mm(kv[:, HD:], chances.astype(BF), TN)
        return (newest, summed, total)

    largest, summed, total = lax.fori_loop(
        0,
        i + 1,
        step,
        (
            jnp.full((1, 2 * QB), MASKED, F32),
            jnp.zeros((1, 2 * QB), F32),
            jnp.zeros((HD, 2 * QB), F32),
        ),
    )
    total = total / summed
    out_ref[...] = jnp.concatenate([total[:, :QB], total[:, QB:]], axis=0).T.astype(BF)
    lse_ref[0] = largest + jnp.log(summed)


def attend(qkv, start):
    return pl.pallas_call(
        attend_kernel,
        grid=(NQ,),
        in_specs=[
            pl.BlockSpec((QB, 2 * HD), lambda i: (i, 0)),
            pl.BlockSpec((SEQ, 2 * HD), lambda i: (0, 1)),
            pl.BlockSpec((1, 1, QB), lambda i: (i, 0, 0)),
        ],
        out_specs=[
            pl.BlockSpec((QB, 2 * HD), lambda i: (i, 0)),
            pl.BlockSpec((1, 1, 2 * QB), lambda i: (i, 0, 0)),
        ],
        out_shape=[
            jax.ShapeDtypeStruct((SEQ, 2 * HD), BF),
            jax.ShapeDtypeStruct((NQ, 1, 2 * QB), F32),
        ],
        compiler_params=pltpu.CompilerParams(vmem_limit_bytes=VMEM),
    )(qkv, qkv, start)


def attend_back_kernel(
    q_ref,
    kv_ref,
    grad_ref,
    start_ref,
    lse_ref,
    cos_t_ref,
    sin_t_ref,
    cos_ref,
    sin_ref,
    out_ref,
    chances_ref,
    pressure_ref,
    dk_ref,
    dv_ref,
):
    i = pl.program_id(0)

    @pl.when(i == 0)
    def clear():
        dk_ref[...] = jnp.zeros_like(dk_ref)
        dv_ref[...] = jnp.zeros_like(dv_ref)

    q2 = stacked_heads(q_ref[...])
    grad2 = stacked_heads(grad_ref[...])
    start_row = jnp.concatenate([start_ref[0], start_ref[0]], axis=1)
    lse = lse_ref[0]

    def first(j, delta):
        rows = pl.ds(pl.multiple_of(j * QB, QB), QB)
        kv = kv_ref[rows, :]
        scores = mm(kv[:, :HD], q2, NT)
        chances = jnp.where(allowed_keys(j, i, start_row), jnp.exp(scores - lse), 0.0)
        pressure = mm(kv[:, HD:], grad2, NT)
        chances_ref[rows, :] = chances
        pressure_ref[rows, :] = pressure
        return delta + jnp.sum(chances * pressure, axis=0, keepdims=True)

    delta = lax.fori_loop(0, i + 1, first, jnp.zeros((1, 2 * QB), F32))

    def second(j, total):
        rows = pl.ds(pl.multiple_of(j * QB, QB), QB)
        chances = chances_ref[rows, :]
        score_grad = (chances * (pressure_ref[rows, :] - delta)).astype(BF)
        dv_ref[rows, :] += mm(chances.astype(BF), grad2)
        dk_ref[rows, :] += mm(score_grad, q2)
        return total + mm(kv_ref[rows, :HD], score_grad, TN)

    total = lax.fori_loop(0, i + 1, second, jnp.zeros((HD, 2 * QB), F32)) * SCALE
    cosine, sine = cos_t_ref[...], sin_t_ref[...]
    half = HD // 2
    parts = []
    for head in range(2):
        front = total[:half, head * QB : (head + 1) * QB]
        back = total[half:, head * QB : (head + 1) * QB]
        parts += [front * cosine + back * sine, back * cosine - front * sine]
    query_rows = pl.ds(pl.multiple_of(i * QB, QB), QB)
    out_ref[query_rows, : 2 * HD] = jnp.concatenate(parts, axis=0).T.astype(BF)

    @pl.when(i == NQ - 1)
    def finish():
        for j in range(NQ):
            rows = slice(j * QB, (j + 1) * QB)
            dk = dk_ref[rows, :]
            swapped = jnp.concatenate([dk[:, half:], dk[:, :half]], axis=1)
            dk = dk * cos_ref[rows, :] - swapped * sin_ref[rows, :]
            out_ref[rows, 2 * HD :] = jnp.concatenate([dk, dv_ref[rows, :]], axis=1).astype(BF)


def attend_back(qkv, grad, start, lse, cos_t, sin_t, cos, sin):
    whole = lambda width, at: pl.BlockSpec((SEQ, width), lambda i: (0, at))
    block = pl.BlockSpec((QB, 2 * HD), lambda i: (i, 0))
    table = pl.BlockSpec((HD // 2, QB), lambda i: (0, i))
    return pl.pallas_call(
        attend_back_kernel,
        grid=(NQ,),
        in_specs=[
            block,
            whole(2 * HD, 1),
            block,
            pl.BlockSpec((1, 1, QB), lambda i: (i, 0, 0)),
            pl.BlockSpec((1, 1, 2 * QB), lambda i: (i, 0, 0)),
            table,
            table,
            whole(HD, 0),
            whole(HD, 0),
        ],
        out_specs=whole(4 * HD, 0),
        out_shape=jax.ShapeDtypeStruct((SEQ, 4 * HD), BF),
        scratch_shapes=[
            pltpu.VMEM((SEQ, 2 * QB), F32),
            pltpu.VMEM((SEQ, 2 * QB), F32),
            pltpu.VMEM((SEQ, HD), F32),
            pltpu.VMEM((SEQ, HD), F32),
        ],
        compiler_params=pltpu.CompilerParams(vmem_limit_bytes=VMEM),
    )(qkv, qkv, grad, start, lse, cos_t, sin_t, cos, sin)


def hi_lo(value):
    high = value.astype(BF).astype(F32)
    rest = value - high
    middle = rest.astype(BF).astype(F32)
    return high, middle, (rest - middle).astype(BF).astype(F32)


def route_kernel(
    mixed_ref, tokens_ref, out_ref, small_ref, gains_ref, chosen_ref, middle_ref, rows_ref, gates_ref
):
    mixed = jnp.concatenate([mixed_ref[g] for g in range(NR)], axis=1)
    middle = tokens_ref[...].astype(F32) + mm(mixed, out_ref[...])
    middle_ref[...] = middle
    inverse = lax.rsqrt(jnp.mean(middle * middle, axis=-1, keepdims=True) + EPSILON)
    normed = (middle * inverse * gains_ref[1:2, :]).astype(BF)
    rows_ref[:, :D] = normed
    chosen = chosen_ref[...] > 0.0
    logits = jnp.where(chosen, mm(normed, small_ref[...]), MASKED)
    powers = jnp.exp(logits - jnp.max(logits, axis=-1, keepdims=True))
    powers = jnp.where(chosen, powers, 0.0)
    gates = powers / jnp.sum(powers, axis=-1, keepdims=True)
    gates_ref[...] = gates
    high, middle_part, low = hi_lo(gates)
    rows_ref[:, D:] = (high + pltpu.roll(middle_part, 32, 1) + pltpu.roll(low, 64, 1)).astype(BF)


def route(mixed, tokens, gathered, gains, chosen):
    fixed = lambda rows, width, at: pl.BlockSpec((rows, width), lambda i: (0, at))
    return pl.pallas_call(
        route_kernel,
        grid=(1,),
        in_specs=[
            pl.BlockSpec((NR, TOK, 128), lambda i: (0, 0, 0)),
            fixed(TOK, D, 0),
            fixed(D, D, 2),
            fixed(D, 128, 24),
            fixed(8, D, 0),
            fixed(TOK, 128, 0),
        ],
        out_specs=[fixed(TOK, D, 0), fixed(TOK, D + 128, 0), fixed(TOK, 128, 0)],
        out_shape=[
            jax.ShapeDtypeStruct((TOK, D), F32),
            jax.ShapeDtypeStruct((TOK, D + 128), BF),
            jax.ShapeDtypeStruct((TOK, 128), F32),
        ],
        compiler_params=pltpu.CompilerParams(vmem_limit_bytes=VMEM),
    )(mixed, tokens, gathered, gathered, gains, chosen)


def expert_kernel(
    rows_ref,
    cot_ref,
    slots_ref,
    own_ref,
    weight_ref,
    combined_ref,
    back_ref,
    grad_ref,
    x_ref,
    g_ref,
    hidden_ref,
    dgate_ref,
    dup_ref,
):
    step = pl.program_id(0)

    @pl.when(step < CHUNKS)
    def forward_backward():
        row_index = lax.broadcasted_iota(jnp.int32, (SLOTS, 128), 0)
        lane_index = lax.broadcasted_iota(jnp.int32, (SLOTS, 128), 1)
        slot_index = lax.broadcasted_iota(jnp.int32, (SLOTS, TOK), 0).astype(F32)
        x_parts, cot_parts, all_picks, weighted = [[], []], [[], []], [], []
        for b in range(BLOCKS):
            tokens = slice(b * TOK, (b + 1) * TOK)
            picks = jnp.concatenate(
                [(slots_ref[e, 0, b : b + 1, :] == slot_index).astype(F32) for e in range(2)], axis=0
            ).astype(BF)
            all_picks.append(picks)
            picked = mm(picks, rows_ref[tokens, :])
            picked_cot = mm(picks, cot_ref[tokens, :D])
            for e in range(2):
                x_parts[e].append(picked[e * SLOTS : (e + 1) * SLOTS])
                cot_parts[e].append(picked_cot[e * SLOTS : (e + 1) * SLOTS])
        here = pl.ds(pl.multiple_of(step * CHUNK_ROWS, CHUNK_ROWS), CHUNK_ROWS)
        for e in range(2):
            both = jnp.concatenate(x_parts[e], axis=0)
            gates = jnp.sum(both[:, D:] * own_ref[e], axis=1, keepdims=True)
            x = both[:, :D].astype(BF)
            cot = jnp.concatenate(cot_parts[e], axis=0)
            gate_w, up_w, down_w = weight_ref[e, 0], weight_ref[e, 1], weight_ref[e, 2]
            gate = mm(x, gate_w)
            up = mm(x, up_w)
            sigmoid = 1.0 / (1.0 + jnp.exp(-gate))
            silu = gate * sigmoid
            hidden = (silu * up).astype(BF)
            grad_out = (gates * cot).astype(BF)
            grad_hidden = mm(grad_out, down_w)
            grad_gate = (grad_hidden * up * sigmoid * (1.0 + gate * (1.0 - sigmoid))).astype(BF)
            grad_up = (grad_hidden * silu).astype(BF)
            x_ref[e, here, :] = x
            g_ref[e, here, :] = grad_out
            hidden_ref[e, here, :] = hidden
            dgate_ref[e, here, :] = grad_gate
            dup_ref[e, here, :] = grad_up
            produced = mm(hidden, down_w, NT).astype(BF).astype(F32)
            weighted.append((gates * produced).astype(BF))
            gate_grads = jnp.sum(cot * produced, axis=1, keepdims=True)
            grad_in = mm(grad_gate, gate_w, NT) + mm(grad_up, up_w, NT)
            for b in range(BLOCKS):
                block = slice(b * SLOTS, (b + 1) * SLOTS)
                row = jnp.sum(
                    jnp.where(row_index == lane_index, gate_grads[block], 0.0), axis=0, keepdims=True
                )
                spare = jnp.zeros((SLOTS, 128), F32)
                for place, part in enumerate(hi_lo(row)):
                    spare = jnp.where(row_index == 60 + place, part, spare)
                back_ref[b, e, :, :128] = (grad_in[block, :128] + spare).astype(BF)
                back_ref[b, e, :, 128:] = grad_in[block, 128:].astype(BF)
        for b in range(BLOCKS):
            block = slice(b * SLOTS, (b + 1) * SLOTS)
            rows = jnp.concatenate([weighted[0][block], weighted[1][block]], axis=0)
            combined_ref[b % 2, 0, b // 2] = mm(all_picks[b], rows, TN).astype(BF)

    for e in range(2):
        for n, (left, right) in enumerate(((x_ref, dgate_ref), (x_ref, dup_ref), (g_ref, hidden_ref))):

            @pl.when(step == CHUNKS + 3 * e + n)
            def weight_grads(left=left, right=right, e=e):
                grad_ref[0, 0] = mm(left[e], right[e], TN).astype(BF)


def run_experts(rows, cot, slots, own, experts):
    chunk = lambda i: jnp.minimum(i, CHUNKS - 1)
    after = lambda i: jnp.maximum(i - CHUNKS, 0)
    taken = pl.BlockSpec((BLOCKS * TOK, D + 128), lambda i: (chunk(i), 0))
    made = pl.BlockSpec((BLOCKS, 2, SLOTS, D), lambda i: (chunk(i), 0, 0, 0))
    return pl.pallas_call(
        expert_kernel,
        grid=(CHUNKS + 6,),
        in_specs=[
            taken,
            taken,
            pl.BlockSpec((2, 1, BLOCKS, TOK), lambda i: (0, chunk(i), 0, 0)),
            pl.BlockSpec((2, 1, 128), lambda i: (0, 0, 0)),
            pl.BlockSpec((2, 3, D, FF), lambda i: (0, 0, 0, 0), pipeline_mode=pl.Buffered(1)),
        ],
        out_specs=[
            pl.BlockSpec((2, 1, 2, TOK, D), lambda i: (0, chunk(i), 0, 0, 0)),
            made,
            pl.BlockSpec((1, 1, D, FF), lambda i: (after(i) // 3, after(i) % 3, 0, 0)),
        ],
        out_shape=[
            jax.ShapeDtypeStruct((2, 4, 2, TOK, D), BF),
            jax.ShapeDtypeStruct((NS, 2, SLOTS, D), BF),
            jax.ShapeDtypeStruct((2, 3, D, FF), BF),
        ],
        scratch_shapes=[
            pltpu.VMEM((2, NS * SLOTS, D), BF),
            pltpu.VMEM((2, NS * SLOTS, D), BF),
            pltpu.VMEM((2, NS * SLOTS, FF), BF),
            pltpu.VMEM((2, NS * SLOTS, FF), BF),
            pltpu.VMEM((2, NS * SLOTS, FF), BF),
        ],
        compiler_params=pltpu.CompilerParams(vmem_limit_bytes=VMEM),
    )(rows, cot, slots, own, experts)


def token_kernel(
    back_ref,
    spots_ref,
    spread_ref,
    gate_rows_ref,
    gates_ref,
    cot_ref,
    middle_ref,
    normed_ref,
    gains_ref,
    small_ref,
    out_ref,
    mixed_ref,
    middle_grad_ref,
    mixed_grad_ref,
    dense_ref,
):
    spots = spots_ref[...]
    rows = mm(spots, back_ref[...])
    gate_grad = jnp.zeros((TOK, 128), F32)
    for p in range(3):
        gate_grad += mm(spots * gate_rows_ref[p : p + 1, :], spread_ref[...])
    gates = gates_ref[...]
    chosen_grad = gates * (gate_grad - jnp.sum(gates * gate_grad, axis=-1, keepdims=True))
    logit_grad = chosen_grad.astype(BF)
    normed_grad = mm(logit_grad, small_ref[...], NT) + rows
    middle = middle_ref[...]
    inverse = lax.rsqrt(jnp.mean(middle * middle, axis=-1, keepdims=True) + EPSILON)
    hat = middle * inverse
    scaled = normed_grad * gains_ref[1:2, :]
    middle_grad = cot_ref[...].astype(F32) + inverse * (
        scaled - hat * jnp.mean(scaled * hat, axis=-1, keepdims=True)
    )
    middle_grad_ref[...] = middle_grad
    branch = middle_grad.astype(BF)
    mixed_grad = mm(branch, out_ref[...], NT).astype(BF)
    for g in range(NR):
        mixed_grad_ref[g] = mixed_grad[:, g * 128 : (g + 1) * 128]
    gain_grad = jnp.sum(normed_grad * hat, axis=0, keepdims=True)
    lane = lax.broadcasted_iota(jnp.int32, (D, 128), 1)
    gain_column = jnp.broadcast_to(gain_grad, (128, D)).T
    router_grad = mm(normed_ref[...], logit_grad, TN)
    dense_ref[:, D:] = jnp.where(lane == 32, gain_column, router_grad).astype(BF)
    for g in range(NR):
        dense_ref[g * 128 : (g + 1) * 128, :D] = mm(mixed_ref[g], branch, TN).astype(BF)


def token_back(back, spots, spread, gate_rows, gates, cot, middle, rows, gains, gathered, mixed):
    fixed = lambda count, width, at=0: pl.BlockSpec((count, width), lambda i: (0, at))
    return pl.pallas_call(
        token_kernel,
        grid=(1,),
        in_specs=[
            fixed(E * SLOTS, D),
            fixed(TOK, E * SLOTS),
            fixed(E * SLOTS, 128),
            fixed(3, E * SLOTS),
            fixed(TOK, 128),
            fixed(TOK, D),
            fixed(TOK, D),
            fixed(TOK, D),
            fixed(8, D),
            fixed(D, 128, 24),
            fixed(D, D, 2),
            pl.BlockSpec((NR, TOK, 128), lambda i: (0, 0, 0)),
        ],
        out_specs=[
            fixed(TOK, D),
            pl.BlockSpec((NR, TOK, 128), lambda i: (0, 0, 0)),
            fixed(D, D + 128),
        ],
        out_shape=[
            jax.ShapeDtypeStruct((TOK, D), F32),
            jax.ShapeDtypeStruct((NR, TOK, 128), BF),
            jax.ShapeDtypeStruct((D, D + 128), BF),
        ],
        compiler_params=pltpu.CompilerParams(vmem_limit_bytes=VMEM),
    )(back, spots, spread, gate_rows, gates, cot, middle, rows, gains, gathered, gathered, mixed)


def after(value, *others):
    return lax.optimization_barrier((value,) + others)[0]


def heads_kernel(parts_ref, query_ref, key_ref, value_ref, gain_ref, dq_ref, dk_ref, dv_ref, norm_ref):
    total = jnp.zeros((64, 128), F32)
    for pair in range(NR // 2):
        first, second = parts_ref[2 * pair, :64].astype(F32), parts_ref[2 * pair + 1, :64].astype(F32)
        lanes = slice(pair * 128, (pair + 1) * 128)
        for at, part in ((2 * pair, first), (2 * pair + 1, second)):
            wide = slice(at * 128, (at + 1) * 128)
            dq_ref[:, wide] = part[:, :128]
            total += part[:, :128] * query_ref[:, wide].astype(F32)
        dk = jnp.concatenate([first[:, 128:192], second[:, 128:192]], axis=1)
        dv = jnp.concatenate([first[:, 192:], second[:, 192:]], axis=1)
        dk_ref[:, lanes] = dk
        dv_ref[:, lanes] = dv
        total += dk * key_ref[:, lanes].astype(F32) + dv * value_ref[:, lanes].astype(F32)
    norm_ref[...] = jnp.sum(total, axis=1, keepdims=True) / gain_ref[...]


def finish_heads(parts, query_weight, key_matrix, value_matrix, norm_one):
    return pl.pallas_call(
        heads_kernel,
        out_shape=[
            jax.ShapeDtypeStruct((64, 1024), F32),
            jax.ShapeDtypeStruct((64, 512), F32),
            jax.ShapeDtypeStruct((64, 512), F32),
            jax.ShapeDtypeStruct((64, 1), F32),
        ],
    )(parts, query_weight, key_matrix, value_matrix, norm_one.astype(F32)[:, None])


def widen_kernel(places_ref, rows_ref, *refs):
    refs[-1][...] = rows_ref[...].astype(F32)


def widen(rows, places, total=None):
    steps = 4
    block = rows.shape[0] // steps
    given = () if total is None else (total,)
    return pl.pallas_call(
        widen_kernel,
        grid_spec=pltpu.PrefetchScalarGridSpec(
            num_scalar_prefetch=1,
            grid=(steps,),
            in_specs=[pl.BlockSpec((block, FF), lambda i, places: (i, 0))]
            + [pl.BlockSpec(memory_space=pl.ANY)] * len(given),
            out_specs=pl.BlockSpec((block, FF), lambda i, places: (places[i], 0)),
        ),
        out_shape=jax.ShapeDtypeStruct((6 * D, FF), F32),
        input_output_aliases={2: 0} if given else {},
    )(places.astype(jnp.int32), rows, *given)


def exchange(x, bits, axis="replica"):
    return lax.ppermute(x, axis, [(i, i ^ bits) for i in range(lax.axis_size(axis))])


def halves(x, bit):
    half = x.shape[0] // 2
    take = lambda at: lax.dynamic_slice_in_dim(x, at * half, half, 0)
    return take(bit), take(1 - bit)


def in_order(own, other, bit):
    first = jnp.where(bit == 0, own, other)
    return jnp.concatenate([first, jnp.where(bit == 0, other, own)], axis=0)


def add_low(a, b):
    return (a.astype(F32) + b.astype(F32)).astype(BF)


def per_device(
    tokens,
    norm_one,
    query_weight,
    key_matrix,
    value_matrix,
    out_weight,
    norm_two,
    router,
    experts,
    routes,
    segments,
    cotangent,
):
    shard = lax.axis_index("shard")
    replica = lax.axis_index("replica")
    along_x = replica // 2
    side = replica % 2
    low_bit, high_bit = along_x % 2, along_x // 2
    mixed_bit = low_bit ^ high_bit

    grouped = jnp.concatenate(
        [
            query_weight.reshape(64, NR, 128),
            key_matrix.reshape(64, NR, HD),
            value_matrix.reshape(64, NR, HD),
        ],
        axis=2,
    ).reshape(64, 2048)
    small = jnp.concatenate(
        [router, norm_one[:, None], norm_two[:, None], jnp.zeros((64, 94), BF)], axis=1
    )
    gathered = lax.all_gather(
        jnp.concatenate([grouped, out_weight, small], axis=1), "shard", axis=0, tiled=True
    )

    segments_seq = spread_all(segments, "replica", NR).reshape(SEQ)
    first_segment = shard * 3
    count_one = jnp.sum((segments_seq == first_segment).astype(jnp.int32))
    count_two = jnp.sum((segments_seq == first_segment + 1).astype(jnp.int32))
    start = jnp.where(
        segments_seq == first_segment,
        0,
        jnp.where(segments_seq == first_segment + 1, count_one, count_one + count_two),
    ).reshape(NQ, 1, QB)

    chosen = jnp.any(routes[:, :, None] == jnp.arange(128, dtype=jnp.int32), axis=1)
    earlier = jnp.tril(jnp.ones((TOK, TOK), BF), -1)
    slot = jnp.where(chosen, mm(earlier, chosen.astype(BF)), -1.0)
    cot_rows = jnp.concatenate([cotangent, slot.astype(BF)], axis=1)
    cot_all = lax.all_gather(cot_rows, "shard", axis=0, tiled=True)
    spots = slot[:, :E, None] == jnp.arange(SLOTS, dtype=F32)
    spots = spots.astype(BF).reshape(TOK, E * SLOTS)
    spread = (
        jnp.arange(E * SLOTS)[:, None] // SLOTS == jnp.arange(128)[None, :]
    ).astype(BF)

    half = HD // 2
    frequency = 10000.0 ** (-2.0 * jnp.arange(half, dtype=F32) / HD)
    angles = jnp.arange(SEQ, dtype=F32)[:, None] * frequency[None, :]
    cosine, sine = jnp.cos(angles), jnp.sin(angles)
    cos_head = jnp.concatenate([cosine, cosine], axis=1)
    sin_head = jnp.concatenate([-sine, sine], axis=1)
    cos_here = lax.dynamic_slice(cos_head, (replica * TOK, 0), (TOK, HD))
    sin_here = lax.dynamic_slice(sin_head, (replica * TOK, 0), (TOK, HD))
    cos_group = jnp.concatenate(
        [cos_here * SCALE, cos_here * SCALE, cos_here, jnp.ones((TOK, HD), F32)], axis=1
    )
    sin_group = jnp.concatenate(
        [sin_here * SCALE, sin_here * SCALE, sin_here, jnp.zeros((TOK, HD), F32)], axis=1
    )

    tokens_in, start, spots, spread = lax.optimization_barrier((tokens, start, spots, spread))
    qkv_here, normed_one, gains = project(tokens_in, gathered, cos_group, sin_group)
    qkv = split_all(qkv_here, "replica").reshape(SEQ, 256)
    normed_one, qkv = lax.optimization_barrier((normed_one, qkv))
    normed_pair = in_order(normed_one, exchange(normed_one, 1), side)
    mixed_heads, lse = attend(qkv, start)
    mixed = split_all(mixed_heads.reshape(NR, TOK, 128), "replica")
    mixed, normed_pair = lax.optimization_barrier((mixed, normed_pair))
    normed_pairs = [normed_pair] + [exchange(normed_pair, 2 * k) for k in (1, 2, 3)]
    middle, rows_out, gates = route(mixed, tokens, gathered, gains, chosen.astype(F32))

    rows_all = lax.all_gather(rows_out, "shard", axis=0, tiled=True)
    normed_seq = jnp.concatenate(normed_pairs, axis=0)
    own_slots = lax.dynamic_slice(cot_all, (0, D + 2 * shard), (NS * TOK, 2)).astype(F32)
    own_slots = own_slots.T.reshape(2, CHUNKS, BLOCKS, TOK)
    lane = jnp.arange(128)[None, :]
    own = jnp.stack(
        [((lane % E == 2 * shard + e) & (lane < 3 * E)).astype(F32) for e in range(2)]
    )
    combined, grad_in, expert_grad = run_experts(rows_all, cot_all, own_slots, own, experts)
    back = split_all(after(grad_in, normed_seq), "shard")

    rows = expert_grad.reshape(2, 3 * D, FF)
    keep_a, send_a = halves(rows[0], mixed_bit)
    keep_b, send_b = halves(rows[1], high_bit)
    got_a, got_b = exchange(send_a, 2), exchange(send_b, 6)
    keep_a, send_a = halves(add_low(keep_a, got_a), low_bit)
    keep_b, send_b = halves(add_low(keep_b, got_b), low_bit)
    core, row, layer = shard % 2, shard // 2 % 2, shard // 4
    pick = lambda x, at: lax.dynamic_index_in_dim(x, at, 0, keepdims=False)
    from_core = exchange(pick(combined, 1 - core), 1, "shard")
    back, send_a, send_b = lax.optimization_barrier((back, send_a, send_b))
    got_a, got_b = exchange(send_a, 6), exchange(send_b, 2)

    gate_rows = back.reshape(E, SLOTS, D)[:, 60:63, :SLOTS].transpose(1, 0, 2).reshape(3, E * SLOTS)
    middle_grad, mixed_grad, dense = token_back(
        back.reshape(E * SLOTS, D),
        spots,
        spread,
        gate_rows,
        gates,
        cotangent,
        middle,
        rows_out,
        gains,
        gathered,
        mixed,
    )
    grad_heads = split_all(mixed_grad, "replica").reshape(SEQ, 128)
    grad_heads, got_a, got_b = lax.optimization_barrier((grad_heads, got_a, got_b))
    keep_a, send_a = halves(add_low(keep_a, got_a), side)
    keep_b, send_b = halves(add_low(keep_b, got_b), side)
    got = exchange(jnp.concatenate([send_a, send_b], axis=0), 1)
    head_grad = attend_back(
        qkv, grad_heads, start, lse, cosine.T, sine.T, cos_head, sin_head
    )
    head_grad, got = lax.optimization_barrier((head_grad, got))
    own = add_low(jnp.concatenate([keep_a, keep_b], axis=0), got)
    half = own.shape[0] // 2
    other = exchange(own, 1)
    head_rows = jnp.concatenate(
        [
            lax.dynamic_slice_in_dim(head_grad, (along_x ^ k) * 2 * TOK, 2 * TOK, 0)
            for k in range(4)
        ],
        axis=0,
    )
    heads_grad = mm(normed_seq, head_rows, TN).astype(BF)

    dense_parts = split_all(after(dense, grad_heads).reshape(NS, 64, 1152), "shard")
    dense_sum = jnp.sum(dense_parts.astype(F32), axis=0).astype(BF)
    dense_here = split_all(after(dense_sum, heads_grad).reshape(NR, 8, 1152), "replica")
    sums = add_low(pick(combined, core), after(from_core, heads_grad))
    keep = [[pick(sums[:, y], layer), pick(sums[:, y], layer ^ step)] for y, step in ((0, 3), (1, 1))]
    send = [
        jnp.stack([pick(sums[:, y], layer ^ first), pick(sums[:, y], layer ^ 2)])
        for y, first in ((0, 1), (1, 3))
    ]
    layers = [exchange(send[0], 4, "shard"), exchange(send[1], 12, "shard")]

    heads_grad, dense_here, other = lax.optimization_barrier((heads_grad, dense_here, other))
    heads_parts = split_all(heads_grad.reshape(NS, 64, 256), "shard")
    own_a = jnp.concatenate([own[:half], other[:half]], axis=0)
    own_b = jnp.concatenate([own[half:], other[half:]], axis=0)
    other_a, other_b = exchange(own_a, 6), exchange(own_b, 2)
    dense_total = jnp.sum(dense_here.astype(F32), axis=0).astype(BF)
    heads_sum = jnp.sum(heads_parts.astype(F32), axis=0).astype(BF)
    last = jnp.concatenate(
        [heads_sum, dense_total.reshape(36, 256), jnp.zeros((12, 256), BF)], axis=0
    )
    by_token = split_all(after(head_grad, heads_parts).reshape(NR, TOK, 256), "replica")
    by_token, other_a, other_b, *layers = lax.optimization_barrier(
        (by_token, other_a, other_b, *layers)
    )
    own_a = jnp.concatenate([own_a, other_a], axis=0)
    own_b = jnp.concatenate([own_b, other_b], axis=0)
    other_a, other_b = exchange(own_a, 2), exchange(own_b, 6)
    last = spread_all(after(last, by_token), "replica", NR)

    def places(first, bit, low):
        return first + 4 * bit + jnp.stack(
            [2 * at + near for at in (low, 1 - low) for near in (side, 1 - side)]
        )

    expert_total = widen(own_a, places(0, mixed_bit, low_bit))
    expert_total = widen(own_b, places(8, high_bit, low_bit), expert_total)
    last, expert_total = lax.optimization_barrier((last, expert_total))
    keep = [[add_low(keep[y][n], layers[y][n]) for n in range(2)] for y in range(2)]
    layers = [exchange(keep[0][1], 12, "shard"), exchange(keep[1][1], 4, "shard")]
    query_grad, key_grad, value_grad, norm_one_grad = finish_heads(
        last, query_weight, key_matrix, value_matrix, norm_one
    )
    dense_last = last[:, 64:100].reshape(64, 1152).astype(F32)

    layers = [after(part, last) for part in layers]
    normed_grad = mm(by_token.transpose(1, 0, 2).reshape(TOK, 2048), gathered[:, :2048], NT)
    tokens_wide = tokens.astype(F32)
    inverse = lax.rsqrt(jnp.mean(tokens_wide * tokens_wide, axis=-1, keepdims=True) + EPSILON)
    hat = tokens_wide * inverse
    scaled = normed_grad * gains[0:1]
    tokens_grad = (
        middle_grad + inverse * (scaled - hat * jnp.mean(scaled * hat, axis=-1, keepdims=True))
    ).astype(BF)

    sides = [add_low(keep[y][0], layers[y]) for y in range(2)]
    own_side = jnp.where(row == 0, sides[0], sides[1])
    from_side = exchange(jnp.where(row == 0, sides[1], sides[0]), 2, "shard")
    from_side = after(from_side, tokens_grad)
    layer_out = (middle + own_side.astype(F32) + from_side.astype(F32)).astype(BF)
    expert_total = widen(other_a, places(0, 1 - mixed_bit, 1 - low_bit), expert_total)
    expert_total = widen(other_b, places(8, 1 - high_bit, 1 - low_bit), expert_total)
    expert_total = expert_total.reshape(2, 3, D, FF)
    return (
        layer_out,
        tokens_grad,
        norm_one_grad[:, 0],
        query_grad,
        key_grad,
        value_grad,
        dense_last[:, :1024],
        dense_last[:, 1056],
        dense_last[:, 1024:1056],
        expert_total,
    )


def solution(mesh):
    return jax.shard_map(
        per_device,
        mesh=mesh,
        in_specs=(
            P(("shard", "replica"), None),
            P("shard"),
            P("shard", None),
            P("shard", None),
            P("shard", None),
            P("shard", None),
            P("shard"),
            P("shard", None),
            P("shard", None, None, None),
            P(("shard", "replica"), None),
            P(("shard", "replica")),
            P(("shard", "replica"), None),
        ),
        out_specs=(
            P(("shard", "replica"), None),
            P(("shard", "replica"), None),
            P("shard"),
            P("shard", None),
            P("shard", None),
            P("shard", None),
            P("shard", None),
            P("shard"),
            P("shard", None),
            P("shard", None, None, None),
        ),
        check_vma=False,
    )
```

```python
import jax
import jax.numpy as jnp
from jax import lax
from jax.experimental import pallas as pl
from jax.experimental.pallas import tpu as pltpu
from jax.sharding import PartitionSpec as P

D = 1024
H = 16
KVH = 8
HD = 64
FF = 512
E = 32
TOP = 8
SEQ = 1536
TOK = 192
NS = 16
NR = 8
SLOTS = 64
QB = 256
NQ = SEQ // QB
EPSILON = 1e-06
MASKED = -1e30
SCALE = HD ** (-0.5)
BLOCKS = 4
CHUNKS = NS // BLOCKS
CHUNK_ROWS = BLOCKS * SLOTS
VMEM = 56 * 1024 * 1024
BF = jnp.bfloat16
F32 = jnp.float32

NT = (((1,), (1,)), ((), ()))
TN = (((0,), (0,)), ((), ()))


def mm(a, b, dims=(((1,), (0,)), ((), ()))):
    return lax.dot_general(a, b, dims, preferred_element_type=F32)


def split_all(x, axis):
    return lax.all_to_all(x, axis, 0, 0, tiled=True)


def spread_all(x, axis, count):
    return split_all(jnp.broadcast_to(x[None], (count,) + x.shape), axis)


def stacked_heads(block):
    return jnp.concatenate([block[:, :HD], block[:, HD:]], axis=0)


def allowed_keys(key_block, query_block, start_row):
    key_index = lax.broadcasted_iota(jnp.int32, (QB, 2 * QB), 0) + key_block * QB
    column = lax.broadcasted_iota(jnp.int32, (1, 2 * QB), 1)
    query_row = jnp.where(column >= QB, column - QB, column) + query_block * QB
    return (key_index >= start_row) & (key_index <= query_row)


def rotary_swap(value):
    lane = lax.broadcasted_iota(jnp.int32, value.shape, 1) % HD
    width = value.shape[1]
    return jnp.where(
        lane < HD // 2,
        pltpu.roll(value, width - HD // 2, 1),
        pltpu.roll(value, HD // 2, 1),
    )


def project_kernel(tokens_ref, weight_ref, small_ref, cos_ref, sin_ref, qkv_ref, normed_ref, gains_ref):
    @pl.when(pl.program_id(0) == 0)
    def norm():
        gains = small_ref[...].astype(F32).T[32:40]
        gains_ref[...] = gains
        wide = tokens_ref[...].astype(F32)
        inverse = lax.rsqrt(jnp.mean(wide * wide, axis=-1, keepdims=True) + EPSILON)
        normed_ref[...] = (wide * inverse * gains[0:1]).astype(BF)

    raw = mm(normed_ref[...], weight_ref[...])
    qkv_ref[0] = (raw * cos_ref[...] + rotary_swap(raw) * sin_ref[...]).astype(BF)


def project(tokens, gathered, cos, sin):
    fixed = lambda rows, width, at: pl.BlockSpec((rows, width), lambda g: (0, at))
    return pl.pallas_call(
        project_kernel,
        grid=(NR,),
        in_specs=[
            fixed(TOK, D, 0),
            pl.BlockSpec((D, 256), lambda g: (0, g)),
            fixed(D, 128, 24),
            fixed(TOK, 256, 0),
            fixed(TOK, 256, 0),
        ],
        out_specs=[
            pl.BlockSpec((1, TOK, 256), lambda g: (g, 0, 0)),
            fixed(TOK, D, 0),
            fixed(8, D, 0),
        ],
        out_shape=[
            jax.ShapeDtypeStruct((NR, TOK, 256), BF),
            jax.ShapeDtypeStruct((TOK, D), BF),
            jax.ShapeDtypeStruct((8, D), F32),
        ],
        compiler_params=pltpu.CompilerParams(vmem_limit_bytes=VMEM),
    )(tokens, gathered, gathered, cos, sin)


def attend_kernel(q_ref, kv_ref, start_ref, out_ref, lse_ref):
    i = pl.program_id(0)
    q2 = stacked_heads(q_ref[...])
    start_row = jnp.concatenate([start_ref[0], start_ref[0]], axis=1)

    def step(j, carry):
        largest, summed, total = carry
        kv = kv_ref[pl.ds(pl.multiple_of(j * QB, QB), QB), :]
        scores = mm(kv[:, :HD], q2, NT)
        scores = jnp.where(allowed_keys(j, i, start_row), scores, MASKED)
        newest = jnp.maximum(largest, jnp.max(scores, axis=0, keepdims=True))
        chances = jnp.exp(scores - newest)
        factor = jnp.exp(largest - newest)
        summed = summed * factor + jnp.sum(chances, axis=0, keepdims=True)
        total = total * factor + mm(kv[:, HD:], chances.astype(BF), TN)
        return (newest, summed, total)

    largest, summed, total = lax.fori_loop(
        0,
        i + 1,
        step,
        (
            jnp.full((1, 2 * QB), MASKED, F32),
            jnp.zeros((1, 2 * QB), F32),
            jnp.zeros((HD, 2 * QB), F32),
        ),
    )
    total = total / summed
    out_ref[...] = jnp.concatenate([total[:, :QB], total[:, QB:]], axis=0).T.astype(BF)
    lse_ref[0] = largest + jnp.log(summed)


def attend(qkv, start):
    return pl.pallas_call(
        attend_kernel,
        grid=(NQ,),
        in_specs=[
            pl.BlockSpec((QB, 2 * HD), lambda i: (i, 0)),
            pl.BlockSpec((SEQ, 2 * HD), lambda i: (0, 1)),
            pl.BlockSpec((1, 1, QB), lambda i: (i, 0, 0)),
        ],
        out_specs=[
            pl.BlockSpec((QB, 2 * HD), lambda i: (i, 0)),
            pl.BlockSpec((1, 1, 2 * QB), lambda i: (i, 0, 0)),
        ],
        out_shape=[
            jax.ShapeDtypeStruct((SEQ, 2 * HD), BF),
            jax.ShapeDtypeStruct((NQ, 1, 2 * QB), F32),
        ],
        compiler_params=pltpu.CompilerParams(vmem_limit_bytes=VMEM),
    )(qkv, qkv, start)


def attend_back_kernel(
    q_ref,
    kv_ref,
    grad_ref,
    start_ref,
    lse_ref,
    cos_t_ref,
    sin_t_ref,
    cos_ref,
    sin_ref,
    out_ref,
    chances_ref,
    pressure_ref,
    dk_ref,
    dv_ref,
):
    i = pl.program_id(0)

    @pl.when(i == 0)
    def clear():
        dk_ref[...] = jnp.zeros_like(dk_ref)
        dv_ref[...] = jnp.zeros_like(dv_ref)

    q2 = stacked_heads(q_ref[...])
    grad2 = stacked_heads(grad_ref[...])
    start_row = jnp.concatenate([start_ref[0], start_ref[0]], axis=1)
    lse = lse_ref[0]

    def first(j, delta):
        rows = pl.ds(pl.multiple_of(j * QB, QB), QB)
        kv = kv_ref[rows, :]
        scores = mm(kv[:, :HD], q2, NT)
        chances = jnp.where(allowed_keys(j, i, start_row), jnp.exp(scores - lse), 0.0)
        pressure = mm(kv[:, HD:], grad2, NT)
        chances_ref[rows, :] = chances
        pressure_ref[rows, :] = pressure
        return delta + jnp.sum(chances * pressure, axis=0, keepdims=True)

    delta = lax.fori_loop(0, i + 1, first, jnp.zeros((1, 2 * QB), F32))

    def second(j, total):
        rows = pl.ds(pl.multiple_of(j * QB, QB), QB)
        chances = chances_ref[rows, :]
        score_grad = (chances * (pressure_ref[rows, :] - delta)).astype(BF)
        dv_ref[rows, :] += mm(chances.astype(BF), grad2)
        dk_ref[rows, :] += mm(score_grad, q2)
        return total + mm(kv_ref[rows, :HD], score_grad, TN)

    total = lax.fori_loop(0, i + 1, second, jnp.zeros((HD, 2 * QB), F32)) * SCALE
    cosine, sine = cos_t_ref[...], sin_t_ref[...]
    half = HD // 2
    parts = []
    for head in range(2):
        front = total[:half, head * QB : (head + 1) * QB]
        back = total[half:, head * QB : (head + 1) * QB]
        parts += [front * cosine + back * sine, back * cosine - front * sine]
    query_rows = pl.ds(pl.multiple_of(i * QB, QB), QB)
    out_ref[query_rows, : 2 * HD] = jnp.concatenate(parts, axis=0).T.astype(BF)

    @pl.when(i == NQ - 1)
    def finish():
        for j in range(NQ):
            rows = slice(j * QB, (j + 1) * QB)
            dk = dk_ref[rows, :]
            swapped = jnp.concatenate([dk[:, half:], dk[:, :half]], axis=1)
            dk = dk * cos_ref[rows, :] - swapped * sin_ref[rows, :]
            out_ref[rows, 2 * HD :] = jnp.concatenate([dk, dv_ref[rows, :]], axis=1).astype(BF)


def attend_back(qkv, grad, start, lse, cos_t, sin_t, cos, sin):
    whole = lambda width, at: pl.BlockSpec((SEQ, width), lambda i: (0, at))
    block = pl.BlockSpec((QB, 2 * HD), lambda i: (i, 0))
    table = pl.BlockSpec((HD // 2, QB), lambda i: (0, i))
    return pl.pallas_call(
        attend_back_kernel,
        grid=(NQ,),
        in_specs=[
            block,
            whole(2 * HD, 1),
            block,
            pl.BlockSpec((1, 1, QB), lambda i: (i, 0, 0)),
            pl.BlockSpec((1, 1, 2 * QB), lambda i: (i, 0, 0)),
            table,
            table,
            whole(HD, 0),
            whole(HD, 0),
        ],
        out_specs=whole(4 * HD, 0),
        out_shape=jax.ShapeDtypeStruct((SEQ, 4 * HD), BF),
        scratch_shapes=[
            pltpu.VMEM((SEQ, 2 * QB), F32),
            pltpu.VMEM((SEQ, 2 * QB), F32),
            pltpu.VMEM((SEQ, HD), F32),
            pltpu.VMEM((SEQ, HD), F32),
        ],
        compiler_params=pltpu.CompilerParams(vmem_limit_bytes=VMEM),
    )(qkv, qkv, grad, start, lse, cos_t, sin_t, cos, sin)


def hi_lo(value):
    high = value.astype(BF).astype(F32)
    rest = value - high
    middle = rest.astype(BF).astype(F32)
    return high, middle, (rest - middle).astype(BF).astype(F32)


def route_kernel(
    mixed_ref, tokens_ref, out_ref, small_ref, gains_ref, chosen_ref, middle_ref, rows_ref, gates_ref
):
    mixed = jnp.concatenate([mixed_ref[g] for g in range(NR)], axis=1)
    middle = tokens_ref[...].astype(F32) + mm(mixed, out_ref[...])
    middle_ref[...] = middle
    inverse = lax.rsqrt(jnp.mean(middle * middle, axis=-1, keepdims=True) + EPSILON)
    normed = (middle * inverse * gains_ref[1:2, :]).astype(BF)
    rows_ref[:, :D] = normed
    chosen = chosen_ref[...] > 0.0
    logits = jnp.where(chosen, mm(normed, small_ref[...]), MASKED)
    powers = jnp.exp(logits - jnp.max(logits, axis=-1, keepdims=True))
    powers = jnp.where(chosen, powers, 0.0)
    gates = powers / jnp.sum(powers, axis=-1, keepdims=True)
    gates_ref[...] = gates
    high, middle_part, low = hi_lo(gates)
    rows_ref[:, D:] = (high + pltpu.roll(middle_part, 32, 1) + pltpu.roll(low, 64, 1)).astype(BF)


def route(mixed, tokens, gathered, gains, chosen):
    fixed = lambda rows, width, at: pl.BlockSpec((rows, width), lambda i: (0, at))
    return pl.pallas_call(
        route_kernel,
        grid=(1,),
        in_specs=[
            pl.BlockSpec((NR, TOK, 128), lambda i: (0, 0, 0)),
            fixed(TOK, D, 0),
            fixed(D, D, 2),
            fixed(D, 128, 24),
            fixed(8, D, 0),
            fixed(TOK, 128, 0),
        ],
        out_specs=[fixed(TOK, D, 0), fixed(TOK, D + 128, 0), fixed(TOK, 128, 0)],
        out_shape=[
            jax.ShapeDtypeStruct((TOK, D), F32),
            jax.ShapeDtypeStruct((TOK, D + 128), BF),
            jax.ShapeDtypeStruct((TOK, 128), F32),
        ],
        compiler_params=pltpu.CompilerParams(vmem_limit_bytes=VMEM),
    )(mixed, tokens, gathered, gathered, gains, chosen)


def expert_kernel(
    rows_ref,
    cot_ref,
    slots_ref,
    own_ref,
    weight_ref,
    combined_ref,
    back_ref,
    grad_ref,
    x_ref,
    g_ref,
    hidden_ref,
    dgate_ref,
    dup_ref,
):
    step = pl.program_id(0)

    @pl.when(step < CHUNKS)
    def forward_backward():
        row_index = lax.broadcasted_iota(jnp.int32, (SLOTS, 128), 0)
        lane_index = lax.broadcasted_iota(jnp.int32, (SLOTS, 128), 1)
        slot_index = lax.broadcasted_iota(jnp.int32, (SLOTS, TOK), 0).astype(F32)
        x_parts, cot_parts, all_picks, weighted = [[], []], [[], []], [], []
        for b in range(BLOCKS):
            tokens = slice(b * TOK, (b + 1) * TOK)
            picks = jnp.concatenate(
                [(slots_ref[e, 0, b : b + 1, :] == slot_index).astype(F32) for e in range(2)], axis=0
            ).astype(BF)
            all_picks.append(picks)
            picked = mm(picks, rows_ref[tokens, :])
            picked_cot = mm(picks, cot_ref[tokens, :D])
            for e in range(2):
                x_parts[e].append(picked[e * SLOTS : (e + 1) * SLOTS])
                cot_parts[e].append(picked_cot[e * SLOTS : (e + 1) * SLOTS])
        here = pl.ds(pl.multiple_of(step * CHUNK_ROWS, CHUNK_ROWS), CHUNK_ROWS)
        for e in range(2):
            both = jnp.concatenate(x_parts[e], axis=0)
            gates = jnp.sum(both[:, D:] * own_ref[e], axis=1, keepdims=True)
            x = both[:, :D].astype(BF)
            cot = jnp.concatenate(cot_parts[e], axis=0)
            gate_w, up_w, down_w = weight_ref[e, 0], weight_ref[e, 1], weight_ref[e, 2]
            gate = mm(x, gate_w)
            up = mm(x, up_w)
            sigmoid = 1.0 / (1.0 + jnp.exp(-gate))
            silu = gate * sigmoid
            hidden = (silu * up).astype(BF)
            grad_out = (gates * cot).astype(BF)
            grad_hidden = mm(grad_out, down_w)
            grad_gate = (grad_hidden * up * sigmoid * (1.0 + gate * (1.0 - sigmoid))).astype(BF)
            grad_up = (grad_hidden * silu).astype(BF)
            x_ref[e, here, :] = x
            g_ref[e, here, :] = grad_out
            hidden_ref[e, here, :] = hidden
            dgate_ref[e, here, :] = grad_gate
            dup_ref[e, here, :] = grad_up
            produced = mm(hidden, down_w, NT).astype(BF).astype(F32)
            weighted.append((gates * produced).astype(BF))
            gate_grads = jnp.sum(cot * produced, axis=1, keepdims=True)
            grad_in = mm(grad_gate, gate_w, NT) + mm(grad_up, up_w, NT)
            for b in range(BLOCKS):
                block = slice(b * SLOTS, (b + 1) * SLOTS)
                row = jnp.sum(
                    jnp.where(row_index == lane_index, gate_grads[block], 0.0), axis=0, keepdims=True
                )
                spare = jnp.zeros((SLOTS, 128), F32)
                for place, part in enumerate(hi_lo(row)):
                    spare = jnp.where(row_index == 60 + place, part, spare)
                back_ref[b, e, :, :128] = (grad_in[block, :128] + spare).astype(BF)
                back_ref[b, e, :, 128:] = grad_in[block, 128:].astype(BF)
        for b in range(BLOCKS):
            block = slice(b * SLOTS, (b + 1) * SLOTS)
            rows = jnp.concatenate([weighted[0][block], weighted[1][block]], axis=0)
            combined_ref[b % 2, 0, b // 2] = mm(all_picks[b], rows, TN).astype(BF)

    for e in range(2):
        for n, (left, right) in enumerate(((x_ref, dgate_ref), (x_ref, dup_ref), (g_ref, hidden_ref))):

            @pl.when(step == CHUNKS + 3 * e + n)
            def weight_grads(left=left, right=right, e=e):
                grad_ref[0, 0] = mm(left[e], right[e], TN).astype(BF)


def run_experts(rows, cot, slots, own, experts):
    chunk = lambda i: jnp.minimum(i, CHUNKS - 1)
    after = lambda i: jnp.maximum(i - CHUNKS, 0)
    taken = pl.BlockSpec((BLOCKS * TOK, D + 128), lambda i: (chunk(i), 0))
    made = pl.BlockSpec((BLOCKS, 2, SLOTS, D), lambda i: (chunk(i), 0, 0, 0))
    return pl.pallas_call(
        expert_kernel,
        grid=(CHUNKS + 6,),
        in_specs=[
            taken,
            taken,
            pl.BlockSpec((2, 1, BLOCKS, TOK), lambda i: (0, chunk(i), 0, 0)),
            pl.BlockSpec((2, 1, 128), lambda i: (0, 0, 0)),
            pl.BlockSpec((2, 3, D, FF), lambda i: (0, 0, 0, 0), pipeline_mode=pl.Buffered(1)),
        ],
        out_specs=[
            pl.BlockSpec((2, 1, 2, TOK, D), lambda i: (0, chunk(i), 0, 0, 0)),
            made,
            pl.BlockSpec((1, 1, D, FF), lambda i: (after(i) // 3, after(i) % 3, 0, 0)),
        ],
        out_shape=[
            jax.ShapeDtypeStruct((2, 4, 2, TOK, D), BF),
            jax.ShapeDtypeStruct((NS, 2, SLOTS, D), BF),
            jax.ShapeDtypeStruct((2, 3, D, FF), BF),
        ],
        scratch_shapes=[
            pltpu.VMEM((2, NS * SLOTS, D), BF),
            pltpu.VMEM((2, NS * SLOTS, D), BF),
            pltpu.VMEM((2, NS * SLOTS, FF), BF),
            pltpu.VMEM((2, NS * SLOTS, FF), BF),
            pltpu.VMEM((2, NS * SLOTS, FF), BF),
        ],
        compiler_params=pltpu.CompilerParams(vmem_limit_bytes=VMEM),
    )(rows, cot, slots, own, experts)


def token_kernel(
    back_ref,
    spots_ref,
    spread_ref,
    gate_rows_ref,
    gates_ref,
    cot_ref,
    middle_ref,
    normed_ref,
    gains_ref,
    small_ref,
    out_ref,
    mixed_ref,
    middle_grad_ref,
    mixed_grad_ref,
    dense_ref,
):
    spots = spots_ref[...]
    rows = mm(spots, back_ref[...])
    gate_grad = jnp.zeros((TOK, 128), F32)
    for p in range(3):
        gate_grad += mm(spots * gate_rows_ref[p : p + 1, :], spread_ref[...])
    gates = gates_ref[...]
    chosen_grad = gates * (gate_grad - jnp.sum(gates * gate_grad, axis=-1, keepdims=True))
    logit_grad = chosen_grad.astype(BF)
    normed_grad = mm(logit_grad, small_ref[...], NT) + rows
    middle = middle_ref[...]
    inverse = lax.rsqrt(jnp.mean(middle * middle, axis=-1, keepdims=True) + EPSILON)
    hat = middle * inverse
    scaled = normed_grad * gains_ref[1:2, :]
    middle_grad = cot_ref[...].astype(F32) + inverse * (
        scaled - hat * jnp.mean(scaled * hat, axis=-1, keepdims=True)
    )
    middle_grad_ref[...] = middle_grad
    branch = middle_grad.astype(BF)
    mixed_grad = mm(branch, out_ref[...], NT).astype(BF)
    for g in range(NR):
        mixed_grad_ref[g] = mixed_grad[:, g * 128 : (g + 1) * 128]
    gain_grad = jnp.sum(normed_grad * hat, axis=0, keepdims=True)
    lane = lax.broadcasted_iota(jnp.int32, (D, 128), 1)
    gain_column = jnp.broadcast_to(gain_grad, (128, D)).T
    router_grad = mm(normed_ref[...], logit_grad, TN)
    dense_ref[:, D:] = jnp.where(lane == 32, gain_column, router_grad).astype(BF)
    for g in range(NR):
        dense_ref[g * 128 : (g + 1) * 128, :D] = mm(mixed_ref[g], branch, TN).astype(BF)


def token_back(back, spots, spread, gate_rows, gates, cot, middle, rows, gains, gathered, mixed):
    fixed = lambda count, width, at=0: pl.BlockSpec((count, width), lambda i: (0, at))
    return pl.pallas_call(
        token_kernel,
        grid=(1,),
        in_specs=[
            fixed(E * SLOTS, D),
            fixed(TOK, E * SLOTS),
            fixed(E * SLOTS, 128),
            fixed(3, E * SLOTS),
            fixed(TOK, 128),
            fixed(TOK, D),
            fixed(TOK, D),
            fixed(TOK, D),
            fixed(8, D),
            fixed(D, 128, 24),
            fixed(D, D, 2),
            pl.BlockSpec((NR, TOK, 128), lambda i: (0, 0, 0)),
        ],
        out_specs=[
            fixed(TOK, D),
            pl.BlockSpec((NR, TOK, 128), lambda i: (0, 0, 0)),
            fixed(D, D + 128),
        ],
        out_shape=[
            jax.ShapeDtypeStruct((TOK, D), F32),
            jax.ShapeDtypeStruct((NR, TOK, 128), BF),
            jax.ShapeDtypeStruct((D, D + 128), BF),
        ],
        compiler_params=pltpu.CompilerParams(vmem_limit_bytes=VMEM),
    )(back, spots, spread, gate_rows, gates, cot, middle, rows, gains, gathered, gathered, mixed)


def after(value, *others):
    return lax.optimization_barrier((value,) + others)[0]


def heads_kernel(parts_ref, query_ref, key_ref, value_ref, gain_ref, dq_ref, dk_ref, dv_ref, norm_ref):
    total = jnp.zeros((64, 128), F32)
    for pair in range(NR // 2):
        first, second = parts_ref[2 * pair, :64].astype(F32), parts_ref[2 * pair + 1, :64].astype(F32)
        lanes = slice(pair * 128, (pair + 1) * 128)
        for at, part in ((2 * pair, first), (2 * pair + 1, second)):
            wide = slice(at * 128, (at + 1) * 128)
            dq_ref[:, wide] = part[:, :128]
            total += part[:, :128] * query_ref[:, wide].astype(F32)
        dk = jnp.concatenate([first[:, 128:192], second[:, 128:192]], axis=1)
        dv = jnp.concatenate([first[:, 192:], second[:, 192:]], axis=1)
        dk_ref[:, lanes] = dk
        dv_ref[:, lanes] = dv
        total += dk * key_ref[:, lanes].astype(F32) + dv * value_ref[:, lanes].astype(F32)
    norm_ref[...] = jnp.sum(total, axis=1, keepdims=True) / gain_ref[...]


def finish_heads(parts, query_weight, key_matrix, value_matrix, norm_one):
    return pl.pallas_call(
        heads_kernel,
        out_shape=[
            jax.ShapeDtypeStruct((64, 1024), F32),
            jax.ShapeDtypeStruct((64, 512), F32),
            jax.ShapeDtypeStruct((64, 512), F32),
            jax.ShapeDtypeStruct((64, 1), F32),
        ],
    )(parts, query_weight, key_matrix, value_matrix, norm_one.astype(F32)[:, None])


def widen_kernel(places_ref, *refs):
    step = pl.program_id(0)
    out_ref = refs[-1]
    for n in range(places_ref.shape[0] // 2):

        @pl.when(step // 2 == n)
        def store(n=n):
            out_ref[...] = refs[n][...].astype(F32)


def widen(arrays, places, total=None):
    block = arrays[0].shape[0] // 2
    given = () if total is None else (total,)

    def taken(n):
        return pl.BlockSpec((block, FF), lambda i, places: (jnp.clip(i - 2 * n, 0, 1), 0))

    return pl.pallas_call(
        widen_kernel,
        grid_spec=pltpu.PrefetchScalarGridSpec(
            num_scalar_prefetch=1,
            grid=(2 * len(arrays),),
            in_specs=[taken(n) for n in range(len(arrays))]
            + [pl.BlockSpec(memory_space=pl.ANY)] * len(given),
            out_specs=pl.BlockSpec((block, FF), lambda i, places: (places[i], 0)),
        ),
        out_shape=jax.ShapeDtypeStruct((6 * D, FF), F32),
        input_output_aliases={1 + len(arrays): 0} if given else {},
    )(jnp.concatenate(places).astype(jnp.int32), *arrays, *given)


def exchange(x, bits, axis="replica"):
    return lax.ppermute(x, axis, [(i, i ^ bits) for i in range(lax.axis_size(axis))])


def halves(x, bit):
    half = x.shape[0] // 2
    take = lambda at: lax.dynamic_slice_in_dim(x, at * half, half, 0)
    return take(bit), take(1 - bit)


def in_order(own, other, bit):
    first = jnp.where(bit == 0, own, other)
    return jnp.concatenate([first, jnp.where(bit == 0, other, own)], axis=0)


def add_low(a, b):
    return (a.astype(F32) + b.astype(F32)).astype(BF)


def per_device(
    tokens,
    norm_one,
    query_weight,
    key_matrix,
    value_matrix,
    out_weight,
    norm_two,
    router,
    experts,
    routes,
    segments,
    cotangent,
):
    shard = lax.axis_index("shard")
    replica = lax.axis_index("replica")
    along_x = replica // 2
    side = replica % 2
    low_bit, high_bit = along_x % 2, along_x // 2
    mixed_bit = low_bit ^ high_bit

    grouped = jnp.concatenate(
        [
            query_weight.reshape(64, NR, 128),
            key_matrix.reshape(64, NR, HD),
            value_matrix.reshape(64, NR, HD),
        ],
        axis=2,
    ).reshape(64, 2048)
    small = jnp.concatenate(
        [router, norm_one[:, None], norm_two[:, None], jnp.zeros((64, 94), BF)], axis=1
    )
    gathered = lax.all_gather(
        jnp.concatenate([grouped, out_weight, small], axis=1), "shard", axis=0, tiled=True
    )

    segments_seq = spread_all(segments, "replica", NR).reshape(SEQ)
    first_segment = shard * 3
    count_one = jnp.sum((segments_seq == first_segment).astype(jnp.int32))
    count_two = jnp.sum((segments_seq == first_segment + 1).astype(jnp.int32))
    start = jnp.where(
        segments_seq == first_segment,
        0,
        jnp.where(segments_seq == first_segment + 1, count_one, count_one + count_two),
    ).reshape(NQ, 1, QB)

    chosen = jnp.any(routes[:, :, None] == jnp.arange(128, dtype=jnp.int32), axis=1)
    earlier = jnp.tril(jnp.ones((TOK, TOK), BF), -1)
    slot = jnp.where(chosen, mm(earlier, chosen.astype(BF)), -1.0)
    cot_rows = jnp.concatenate([cotangent, slot.astype(BF)], axis=1)
    cot_all = lax.all_gather(cot_rows, "shard", axis=0, tiled=True)
    spots = slot[:, :E, None] == jnp.arange(SLOTS, dtype=F32)
    spots = spots.astype(BF).reshape(TOK, E * SLOTS)
    spread = (
        jnp.arange(E * SLOTS)[:, None] // SLOTS == jnp.arange(128)[None, :]
    ).astype(BF)

    half = HD // 2
    frequency = 10000.0 ** (-2.0 * jnp.arange(half, dtype=F32) / HD)
    angles = jnp.arange(SEQ, dtype=F32)[:, None] * frequency[None, :]
    cosine, sine = jnp.cos(angles), jnp.sin(angles)
    cos_head = jnp.concatenate([cosine, cosine], axis=1)
    sin_head = jnp.concatenate([-sine, sine], axis=1)
    cos_here = lax.dynamic_slice(cos_head, (replica * TOK, 0), (TOK, HD))
    sin_here = lax.dynamic_slice(sin_head, (replica * TOK, 0), (TOK, HD))
    cos_group = jnp.concatenate(
        [cos_here * SCALE, cos_here * SCALE, cos_here, jnp.ones((TOK, HD), F32)], axis=1
    )
    sin_group = jnp.concatenate(
        [sin_here * SCALE, sin_here * SCALE, sin_here, jnp.zeros((TOK, HD), F32)], axis=1
    )

    tokens_in, start, spots, spread = lax.optimization_barrier((tokens, start, spots, spread))
    qkv_here, normed_one, gains = project(tokens_in, gathered, cos_group, sin_group)
    qkv = split_all(qkv_here, "replica").reshape(SEQ, 256)
    normed_one, qkv = lax.optimization_barrier((normed_one, qkv))
    normed_pair = in_order(normed_one, exchange(normed_one, 1), side)
    mixed_heads, lse = attend(qkv, start)
    mixed = split_all(mixed_heads.reshape(NR, TOK, 128), "replica")
    mixed, normed_pair = lax.optimization_barrier((mixed, normed_pair))
    normed_pairs = [normed_pair] + [exchange(normed_pair, 2 * k) for k in (1, 2, 3)]
    middle, rows_out, gates = route(mixed, tokens, gathered, gains, chosen.astype(F32))

    rows_all = lax.all_gather(rows_out, "shard", axis=0, tiled=True)
    normed_seq = jnp.concatenate(normed_pairs, axis=0)
    own_slots = lax.dynamic_slice(cot_all, (0, D + 2 * shard), (NS * TOK, 2)).astype(F32)
    own_slots = own_slots.T.reshape(2, CHUNKS, BLOCKS, TOK)
    lane = jnp.arange(128)[None, :]
    own = jnp.stack(
        [((lane % E == 2 * shard + e) & (lane < 3 * E)).astype(F32) for e in range(2)]
    )
    combined, grad_in, expert_grad = run_experts(rows_all, cot_all, own_slots, own, experts)
    back = split_all(after(grad_in, normed_seq), "shard")

    rows = expert_grad.reshape(2, 3 * D, FF)
    keep_a, send_a = halves(rows[0], mixed_bit)
    keep_b, send_b = halves(rows[1], high_bit)
    got_a, got_b = exchange(send_a, 2), exchange(send_b, 6)
    keep_a, send_a = halves(add_low(keep_a, got_a), low_bit)
    keep_b, send_b = halves(add_low(keep_b, got_b), low_bit)
    core, row, layer = shard % 2, shard // 2 % 2, shard // 4
    pick = lambda x, at: lax.dynamic_index_in_dim(x, at, 0, keepdims=False)
    for_core = pick(combined, 1 - core)
    back, send_a, send_b, for_core = lax.optimization_barrier((back, send_a, send_b, for_core))
    from_core = exchange(for_core, 1, "shard")
    got_a, got_b = exchange(send_a, 6), exchange(send_b, 2)

    gate_rows = back.reshape(E, SLOTS, D)[:, 60:63, :SLOTS].transpose(1, 0, 2).reshape(3, E * SLOTS)
    middle_grad, mixed_grad, dense = token_back(
        back.reshape(E * SLOTS, D),
        spots,
        spread,
        gate_rows,
        gates,
        cotangent,
        middle,
        rows_out,
        gains,
        gathered,
        mixed,
    )
    grad_heads = split_all(mixed_grad, "replica").reshape(SEQ, 128)
    grad_heads, got_a, got_b = lax.optimization_barrier((grad_heads, got_a, got_b))
    keep_a, send_a = halves(add_low(keep_a, got_a), side)
    keep_b, send_b = halves(add_low(keep_b, got_b), side)
    got = exchange(jnp.concatenate([send_a, send_b], axis=0), 1)
    head_grad = attend_back(
        qkv, grad_heads, start, lse, cosine.T, sine.T, cos_head, sin_head
    )
    head_grad, got = lax.optimization_barrier((head_grad, got))
    own = add_low(jnp.concatenate([keep_a, keep_b], axis=0), got)
    half = own.shape[0] // 2
    other = exchange(own, 1)
    head_rows = jnp.concatenate(
        [
            lax.dynamic_slice_in_dim(head_grad, (along_x ^ k) * 2 * TOK, 2 * TOK, 0)
            for k in range(4)
        ],
        axis=0,
    )
    heads_grad = mm(normed_seq, head_rows, TN).astype(BF)

    dense_parts = split_all(after(dense, grad_heads).reshape(NS, 64, 1152), "shard")
    dense_sum = jnp.sum(dense_parts.astype(F32), axis=0).astype(BF)
    dense_here = split_all(after(dense_sum, heads_grad).reshape(NR, 8, 1152), "replica")
    sums = add_low(pick(combined, core), after(from_core, heads_grad))
    keep = [[pick(sums[:, y], layer), pick(sums[:, y], layer ^ step)] for y, step in ((0, 3), (1, 1))]
    send = [
        jnp.stack([pick(sums[:, y], layer ^ first), pick(sums[:, y], layer ^ 2)])
        for y, first in ((0, 1), (1, 3))
    ]
    layers = [exchange(send[0], 4, "shard"), exchange(send[1], 12, "shard")]

    heads_grad, dense_here, other = lax.optimization_barrier((heads_grad, dense_here, other))
    heads_parts = split_all(heads_grad.reshape(NS, 64, 256), "shard")
    own_a = jnp.concatenate([own[:half], other[:half]], axis=0)
    own_b = jnp.concatenate([own[half:], other[half:]], axis=0)
    other_a, other_b = exchange(own_a, 6), exchange(own_b, 2)
    dense_total = jnp.sum(dense_here.astype(F32), axis=0).astype(BF)
    heads_sum = jnp.sum(heads_parts.astype(F32), axis=0).astype(BF)
    last = jnp.concatenate(
        [heads_sum, dense_total.reshape(36, 256), jnp.zeros((12, 256), BF)], axis=0
    )
    by_token = split_all(after(head_grad, heads_parts).reshape(NR, TOK, 256), "replica")
    layers = [after(part, heads_sum) for part in layers]
    keep = [[add_low(keep[y][n], layers[y][n]) for n in range(2)] for y in range(2)]
    layers = [exchange(keep[0][1], 12, "shard"), exchange(keep[1][1], 4, "shard")]
    next_a, next_b = exchange(after(own_a, heads_sum), 2), exchange(after(own_b, heads_sum), 6)
    by_token, other_a, other_b = lax.optimization_barrier((by_token, other_a, other_b))
    rest_a, rest_b = exchange(other_a, 2), exchange(other_b, 6)
    last = spread_all(after(last, by_token), "replica", NR)

    def places(first, bit, low):
        return first + 4 * bit + 2 * low + jnp.stack([side, 1 - side])

    expert_total = widen(
        [own_a, own_b, other_a, other_b, next_a, next_b],
        [
            places(0, mixed_bit, low_bit),
            places(8, high_bit, low_bit),
            places(0, mixed_bit, 1 - low_bit),
            places(8, high_bit, 1 - low_bit),
            places(0, 1 - mixed_bit, 1 - low_bit),
            places(8, 1 - high_bit, 1 - low_bit),
        ],
    )
    last, expert_total = lax.optimization_barrier((last, expert_total))
    query_grad, key_grad, value_grad, norm_one_grad = finish_heads(
        last, query_weight, key_matrix, value_matrix, norm_one
    )
    dense_last = last[:, 64:100].reshape(64, 1152).astype(F32)

    layers = [after(part, by_token) for part in layers]
    normed_grad = mm(by_token.transpose(1, 0, 2).reshape(TOK, 2048), gathered[:, :2048], NT)
    tokens_wide = tokens.astype(F32)
    inverse = lax.rsqrt(jnp.mean(tokens_wide * tokens_wide, axis=-1, keepdims=True) + EPSILON)
    hat = tokens_wide * inverse
    scaled = normed_grad * gains[0:1]
    tokens_grad = (
        middle_grad + inverse * (scaled - hat * jnp.mean(scaled * hat, axis=-1, keepdims=True))
    ).astype(BF)

    sides = [add_low(keep[y][0], layers[y]) for y in range(2)]
    own_side = jnp.where(row == 0, sides[0], sides[1])
    from_side = exchange(jnp.where(row == 0, sides[1], sides[0]), 2, "shard")
    from_side = after(from_side, tokens_grad)
    layer_out = (middle + own_side.astype(F32) + from_side.astype(F32)).astype(BF)
    expert_total = widen(
        [rest_a, rest_b],
        [places(0, 1 - mixed_bit, low_bit), places(8, 1 - high_bit, low_bit)],
        expert_total,
    )
    expert_total = expert_total.reshape(2, 3, D, FF)
    return (
        layer_out,
        tokens_grad,
        norm_one_grad[:, 0],
        query_grad,
        key_grad,
        value_grad,
        dense_last[:, :1024],
        dense_last[:, 1056],
        dense_last[:, 1024:1056],
        expert_total,
    )


def solution(mesh):
    return jax.shard_map(
        per_device,
        mesh=mesh,
        in_specs=(
            P(("shard", "replica"), None),
            P("shard"),
            P("shard", None),
            P("shard", None),
            P("shard", None),
            P("shard", None),
            P("shard"),
            P("shard", None),
            P("shard", None, None, None),
            P(("shard", "replica"), None),
            P(("shard", "replica")),
            P(("shard", "replica"), None),
        ),
        out_specs=(
            P(("shard", "replica"), None),
            P(("shard", "replica"), None),
            P("shard"),
            P("shard", None),
            P("shard", None),
            P("shard", None),
            P("shard", None),
            P("shard"),
            P("shard", None),
            P("shard", None, None, None),
        ),
        check_vma=False,
    )
```

```python
import jax
import jax.numpy as jnp
from jax import lax
from jax.experimental import pallas as pl
from jax.experimental.pallas import tpu as pltpu
from jax.sharding import PartitionSpec as P

D = 1024
H = 16
KVH = 8
HD = 64
FF = 512
E = 32
TOP = 8
SEQ = 1536
TOK = 192
NS = 16
NR = 8
SLOTS = 64
QB = 256
NQ = SEQ // QB
EPSILON = 1e-06
MASKED = -1e30
SCALE = HD ** (-0.5)
BLOCKS = 4
CHUNKS = NS // BLOCKS
CHUNK_ROWS = BLOCKS * SLOTS
VMEM = 56 * 1024 * 1024
BF = jnp.bfloat16
F32 = jnp.float32

NT = (((1,), (1,)), ((), ()))
TN = (((0,), (0,)), ((), ()))


def mm(a, b, dims=(((1,), (0,)), ((), ()))):
    return lax.dot_general(a, b, dims, preferred_element_type=F32)


def split_all(x, axis):
    return lax.all_to_all(x, axis, 0, 0, tiled=True)


def spread_all(x, axis, count):
    return split_all(jnp.broadcast_to(x[None], (count,) + x.shape), axis)


def stacked_heads(block):
    return jnp.concatenate([block[:, :HD], block[:, HD:]], axis=0)


def allowed_keys(key_block, query_block, start_row):
    key_index = lax.broadcasted_iota(jnp.int32, (QB, 2 * QB), 0) + key_block * QB
    column = lax.broadcasted_iota(jnp.int32, (1, 2 * QB), 1)
    query_row = jnp.where(column >= QB, column - QB, column) + query_block * QB
    return (key_index >= start_row) & (key_index <= query_row)


def rotary_swap(value):
    lane = lax.broadcasted_iota(jnp.int32, value.shape, 1) % HD
    width = value.shape[1]
    return jnp.where(
        lane < HD // 2,
        pltpu.roll(value, width - HD // 2, 1),
        pltpu.roll(value, HD // 2, 1),
    )


def project_kernel(tokens_ref, weight_ref, small_ref, cos_ref, sin_ref, qkv_ref, normed_ref, gains_ref):
    @pl.when(pl.program_id(0) == 0)
    def norm():
        gains = small_ref[...].astype(F32).T[32:40]
        gains_ref[...] = gains
        wide = tokens_ref[...].astype(F32)
        inverse = lax.rsqrt(jnp.mean(wide * wide, axis=-1, keepdims=True) + EPSILON)
        normed_ref[...] = (wide * inverse * gains[0:1]).astype(BF)

    raw = mm(normed_ref[...], weight_ref[...])
    qkv_ref[0] = (raw * cos_ref[...] + rotary_swap(raw) * sin_ref[...]).astype(BF)


def project(tokens, gathered, cos, sin):
    fixed = lambda rows, width, at: pl.BlockSpec((rows, width), lambda g: (0, at))
    return pl.pallas_call(
        project_kernel,
        grid=(NR,),
        in_specs=[
            fixed(TOK, D, 0),
            pl.BlockSpec((D, 256), lambda g: (0, g)),
            fixed(D, 128, 24),
            fixed(TOK, 256, 0),
            fixed(TOK, 256, 0),
        ],
        out_specs=[
            pl.BlockSpec((1, TOK, 256), lambda g: (g, 0, 0)),
            fixed(TOK, D, 0),
            fixed(8, D, 0),
        ],
        out_shape=[
            jax.ShapeDtypeStruct((NR, TOK, 256), BF),
            jax.ShapeDtypeStruct((TOK, D), BF),
            jax.ShapeDtypeStruct((8, D), F32),
        ],
        compiler_params=pltpu.CompilerParams(vmem_limit_bytes=VMEM),
    )(tokens, gathered, gathered, cos, sin)


def attend_kernel(q_ref, kv_ref, start_ref, out_ref, lse_ref):
    i = pl.program_id(0)
    q2 = stacked_heads(q_ref[...])
    start_row = jnp.concatenate([start_ref[0], start_ref[0]], axis=1)

    def step(j, carry):
        largest, summed, total = carry
        kv = kv_ref[pl.ds(pl.multiple_of(j * QB, QB), QB), :]
        scores = mm(kv[:, :HD], q2, NT)
        scores = jnp.where(allowed_keys(j, i, start_row), scores, MASKED)
        newest = jnp.maximum(largest, jnp.max(scores, axis=0, keepdims=True))
        chances = jnp.exp(scores - newest)
        factor = jnp.exp(largest - newest)
        summed = summed * factor + jnp.sum(chances, axis=0, keepdims=True)
        total = total * factor + mm(kv[:, HD:], chances.astype(BF), TN)
        return (newest, summed, total)

    largest, summed, total = lax.fori_loop(
        0,
        i + 1,
        step,
        (
            jnp.full((1, 2 * QB), MASKED, F32),
            jnp.zeros((1, 2 * QB), F32),
            jnp.zeros((HD, 2 * QB), F32),
        ),
    )
    total = total / summed
    out_ref[...] = jnp.concatenate([total[:, :QB], total[:, QB:]], axis=0).T.astype(BF)
    lse_ref[0] = largest + jnp.log(summed)


def attend(qkv, start):
    return pl.pallas_call(
        attend_kernel,
        grid=(NQ,),
        in_specs=[
            pl.BlockSpec((QB, 2 * HD), lambda i: (i, 0)),
            pl.BlockSpec((SEQ, 2 * HD), lambda i: (0, 1)),
            pl.BlockSpec((1, 1, QB), lambda i: (i, 0, 0)),
        ],
        out_specs=[
            pl.BlockSpec((QB, 2 * HD), lambda i: (i, 0)),
            pl.BlockSpec((1, 1, 2 * QB), lambda i: (i, 0, 0)),
        ],
        out_shape=[
            jax.ShapeDtypeStruct((SEQ, 2 * HD), BF),
            jax.ShapeDtypeStruct((NQ, 1, 2 * QB), F32),
        ],
        compiler_params=pltpu.CompilerParams(vmem_limit_bytes=VMEM),
    )(qkv, qkv, start)


def attend_back_kernel(
    q_ref,
    kv_ref,
    grad_ref,
    start_ref,
    lse_ref,
    cos_t_ref,
    sin_t_ref,
    cos_ref,
    sin_ref,
    out_ref,
    chances_ref,
    pressure_ref,
    dk_ref,
    dv_ref,
):
    i = pl.program_id(0)

    @pl.when(i == 0)
    def clear():
        dk_ref[...] = jnp.zeros_like(dk_ref)
        dv_ref[...] = jnp.zeros_like(dv_ref)

    q2 = stacked_heads(q_ref[...])
    grad2 = stacked_heads(grad_ref[...])
    start_row = jnp.concatenate([start_ref[0], start_ref[0]], axis=1)
    lse = lse_ref[0]

    def first(j, delta):
        rows = pl.ds(pl.multiple_of(j * QB, QB), QB)
        kv = kv_ref[rows, :]
        scores = mm(kv[:, :HD], q2, NT)
        chances = jnp.where(allowed_keys(j, i, start_row), jnp.exp(scores - lse), 0.0)
        pressure = mm(kv[:, HD:], grad2, NT)
        chances_ref[rows, :] = chances
        pressure_ref[rows, :] = pressure
        return delta + jnp.sum(chances * pressure, axis=0, keepdims=True)

    delta = lax.fori_loop(0, i + 1, first, jnp.zeros((1, 2 * QB), F32))

    def second(j, total):
        rows = pl.ds(pl.multiple_of(j * QB, QB), QB)
        chances = chances_ref[rows, :]
        score_grad = (chances * (pressure_ref[rows, :] - delta)).astype(BF)
        dv_ref[rows, :] += mm(chances.astype(BF), grad2)
        dk_ref[rows, :] += mm(score_grad, q2)
        return total + mm(kv_ref[rows, :HD], score_grad, TN)

    total = lax.fori_loop(0, i + 1, second, jnp.zeros((HD, 2 * QB), F32)) * SCALE
    cosine, sine = cos_t_ref[...], sin_t_ref[...]
    half = HD // 2
    parts = []
    for head in range(2):
        front = total[:half, head * QB : (head + 1) * QB]
        back = total[half:, head * QB : (head + 1) * QB]
        parts += [front * cosine + back * sine, back * cosine - front * sine]
    query_rows = pl.ds(pl.multiple_of(i * QB, QB), QB)
    out_ref[query_rows, : 2 * HD] = jnp.concatenate(parts, axis=0).T.astype(BF)

    @pl.when(i == NQ - 1)
    def finish():
        for j in range(NQ):
            rows = slice(j * QB, (j + 1) * QB)
            dk = dk_ref[rows, :]
            swapped = jnp.concatenate([dk[:, half:], dk[:, :half]], axis=1)
            dk = dk * cos_ref[rows, :] - swapped * sin_ref[rows, :]
            out_ref[rows, 2 * HD :] = jnp.concatenate([dk, dv_ref[rows, :]], axis=1).astype(BF)


def attend_back(qkv, grad, start, lse, cos_t, sin_t, cos, sin):
    whole = lambda width, at: pl.BlockSpec((SEQ, width), lambda i: (0, at))
    block = pl.BlockSpec((QB, 2 * HD), lambda i: (i, 0))
    table = pl.BlockSpec((HD // 2, QB), lambda i: (0, i))
    return pl.pallas_call(
        attend_back_kernel,
        grid=(NQ,),
        in_specs=[
            block,
            whole(2 * HD, 1),
            block,
            pl.BlockSpec((1, 1, QB), lambda i: (i, 0, 0)),
            pl.BlockSpec((1, 1, 2 * QB), lambda i: (i, 0, 0)),
            table,
            table,
            whole(HD, 0),
            whole(HD, 0),
        ],
        out_specs=whole(4 * HD, 0),
        out_shape=jax.ShapeDtypeStruct((SEQ, 4 * HD), BF),
        scratch_shapes=[
            pltpu.VMEM((SEQ, 2 * QB), F32),
            pltpu.VMEM((SEQ, 2 * QB), F32),
            pltpu.VMEM((SEQ, HD), F32),
            pltpu.VMEM((SEQ, HD), F32),
        ],
        compiler_params=pltpu.CompilerParams(vmem_limit_bytes=VMEM),
    )(qkv, qkv, grad, start, lse, cos_t, sin_t, cos, sin)


def hi_lo(value):
    high = value.astype(BF).astype(F32)
    rest = value - high
    middle = rest.astype(BF).astype(F32)
    return high, middle, (rest - middle).astype(BF).astype(F32)


def route_kernel(
    mixed_ref, tokens_ref, out_ref, small_ref, gains_ref, chosen_ref, middle_ref, rows_ref, gates_ref
):
    mixed = jnp.concatenate([mixed_ref[g] for g in range(NR)], axis=1)
    middle = tokens_ref[...].astype(F32) + mm(mixed, out_ref[...])
    middle_ref[...] = middle
    inverse = lax.rsqrt(jnp.mean(middle * middle, axis=-1, keepdims=True) + EPSILON)
    normed = (middle * inverse * gains_ref[1:2, :]).astype(BF)
    rows_ref[:, :D] = normed
    chosen = chosen_ref[...] > 0.0
    logits = jnp.where(chosen, mm(normed, small_ref[...]), MASKED)
    powers = jnp.exp(logits - jnp.max(logits, axis=-1, keepdims=True))
    powers = jnp.where(chosen, powers, 0.0)
    gates = powers / jnp.sum(powers, axis=-1, keepdims=True)
    gates_ref[...] = gates
    high, middle_part, low = hi_lo(gates)
    rows_ref[:, D:] = (high + pltpu.roll(middle_part, 32, 1) + pltpu.roll(low, 64, 1)).astype(BF)


def route(mixed, tokens, gathered, gains, chosen):
    fixed = lambda rows, width, at: pl.BlockSpec((rows, width), lambda i: (0, at))
    return pl.pallas_call(
        route_kernel,
        grid=(1,),
        in_specs=[
            pl.BlockSpec((NR, TOK, 128), lambda i: (0, 0, 0)),
            fixed(TOK, D, 0),
            fixed(D, D, 2),
            fixed(D, 128, 24),
            fixed(8, D, 0),
            fixed(TOK, 128, 0),
        ],
        out_specs=[fixed(TOK, D, 0), fixed(TOK, D + 128, 0), fixed(TOK, 128, 0)],
        out_shape=[
            jax.ShapeDtypeStruct((TOK, D), F32),
            jax.ShapeDtypeStruct((TOK, D + 128), BF),
            jax.ShapeDtypeStruct((TOK, 128), F32),
        ],
        compiler_params=pltpu.CompilerParams(vmem_limit_bytes=VMEM),
    )(mixed, tokens, gathered, gathered, gains, chosen)


def expert_kernel(
    rows_ref,
    cot_ref,
    slots_ref,
    own_ref,
    weight_ref,
    combined_ref,
    back_ref,
    grad_ref,
    x_ref,
    g_ref,
    hidden_ref,
    dgate_ref,
    dup_ref,
):
    step = pl.program_id(0)

    @pl.when(step < CHUNKS)
    def forward_backward():
        row_index = lax.broadcasted_iota(jnp.int32, (SLOTS, 128), 0)
        lane_index = lax.broadcasted_iota(jnp.int32, (SLOTS, 128), 1)
        slot_index = lax.broadcasted_iota(jnp.int32, (SLOTS, TOK), 0).astype(F32)
        x_parts, cot_parts, all_picks, weighted = [[], []], [[], []], [], []
        for b in range(BLOCKS):
            tokens = slice(b * TOK, (b + 1) * TOK)
            picks = jnp.concatenate(
                [(slots_ref[e, 0, b : b + 1, :] == slot_index).astype(F32) for e in range(2)], axis=0
            ).astype(BF)
            all_picks.append(picks)
            picked = mm(picks, rows_ref[tokens, :])
            picked_cot = mm(picks, cot_ref[tokens, :D])
            for e in range(2):
                x_parts[e].append(picked[e * SLOTS : (e + 1) * SLOTS])
                cot_parts[e].append(picked_cot[e * SLOTS : (e + 1) * SLOTS])
        here = pl.ds(pl.multiple_of(step * CHUNK_ROWS, CHUNK_ROWS), CHUNK_ROWS)
        for e in range(2):
            both = jnp.concatenate(x_parts[e], axis=0)
            gates = jnp.sum(both[:, D:] * own_ref[e], axis=1, keepdims=True)
            x = both[:, :D].astype(BF)
            cot = jnp.concatenate(cot_parts[e], axis=0)
            gate_w, up_w, down_w = weight_ref[e, 0], weight_ref[e, 1], weight_ref[e, 2]
            gate = mm(x, gate_w)
            up = mm(x, up_w)
            sigmoid = 1.0 / (1.0 + jnp.exp(-gate))
            silu = gate * sigmoid
            hidden = (silu * up).astype(BF)
            grad_out = (gates * cot).astype(BF)
            grad_hidden = mm(grad_out, down_w)
            grad_gate = (grad_hidden * up * sigmoid * (1.0 + gate * (1.0 - sigmoid))).astype(BF)
            grad_up = (grad_hidden * silu).astype(BF)
            x_ref[e, here, :] = x
            g_ref[e, here, :] = grad_out
            hidden_ref[e, here, :] = hidden
            dgate_ref[e, here, :] = grad_gate
            dup_ref[e, here, :] = grad_up
            produced = mm(hidden, down_w, NT).astype(BF).astype(F32)
            weighted.append((gates * produced).astype(BF))
            gate_grads = jnp.sum(cot * produced, axis=1, keepdims=True)
            grad_in = mm(grad_gate, gate_w, NT) + mm(grad_up, up_w, NT)
            for b in range(BLOCKS):
                block = slice(b * SLOTS, (b + 1) * SLOTS)
                row = jnp.sum(
                    jnp.where(row_index == lane_index, gate_grads[block], 0.0), axis=0, keepdims=True
                )
                spare = jnp.zeros((SLOTS, 128), F32)
                for place, part in enumerate(hi_lo(row)):
                    spare = jnp.where(row_index == 60 + place, part, spare)
                back_ref[b, e, :, :128] = (grad_in[block, :128] + spare).astype(BF)
                back_ref[b, e, :, 128:] = grad_in[block, 128:].astype(BF)
        for b in range(BLOCKS):
            block = slice(b * SLOTS, (b + 1) * SLOTS)
            rows = jnp.concatenate([weighted[0][block], weighted[1][block]], axis=0)
            combined_ref[b % 2, 0, b // 2] = mm(all_picks[b], rows, TN).astype(BF)

    for e in range(2):
        for n, (left, right) in enumerate(((x_ref, dgate_ref), (x_ref, dup_ref), (g_ref, hidden_ref))):

            @pl.when(step == CHUNKS + 3 * e + n)
            def weight_grads(left=left, right=right, e=e):
                grad_ref[0, 0] = mm(left[e], right[e], TN).astype(BF)


def run_experts(rows, cot, slots, own, experts):
    chunk = lambda i: jnp.minimum(i, CHUNKS - 1)
    after = lambda i: jnp.maximum(i - CHUNKS, 0)
    taken = pl.BlockSpec((BLOCKS * TOK, D + 128), lambda i: (chunk(i), 0))
    made = pl.BlockSpec((BLOCKS, 2, SLOTS, D), lambda i: (chunk(i), 0, 0, 0))
    return pl.pallas_call(
        expert_kernel,
        grid=(CHUNKS + 6,),
        in_specs=[
            taken,
            taken,
            pl.BlockSpec((2, 1, BLOCKS, TOK), lambda i: (0, chunk(i), 0, 0)),
            pl.BlockSpec((2, 1, 128), lambda i: (0, 0, 0)),
            pl.BlockSpec((2, 3, D, FF), lambda i: (0, 0, 0, 0), pipeline_mode=pl.Buffered(1)),
        ],
        out_specs=[
            pl.BlockSpec((2, 1, 2, TOK, D), lambda i: (0, chunk(i), 0, 0, 0)),
            made,
            pl.BlockSpec((1, 1, D, FF), lambda i: (after(i) // 3, after(i) % 3, 0, 0)),
        ],
        out_shape=[
            jax.ShapeDtypeStruct((2, 4, 2, TOK, D), BF),
            jax.ShapeDtypeStruct((NS, 2, SLOTS, D), BF),
            jax.ShapeDtypeStruct((2, 3, D, FF), BF),
        ],
        scratch_shapes=[
            pltpu.VMEM((2, NS * SLOTS, D), BF),
            pltpu.VMEM((2, NS * SLOTS, D), BF),
            pltpu.VMEM((2, NS * SLOTS, FF), BF),
            pltpu.VMEM((2, NS * SLOTS, FF), BF),
            pltpu.VMEM((2, NS * SLOTS, FF), BF),
        ],
        compiler_params=pltpu.CompilerParams(vmem_limit_bytes=VMEM),
    )(rows, cot, slots, own, experts)


def token_kernel(
    back_ref,
    spots_ref,
    spread_ref,
    gate_rows_ref,
    gates_ref,
    cot_ref,
    middle_ref,
    normed_ref,
    gains_ref,
    small_ref,
    out_ref,
    mixed_ref,
    middle_grad_ref,
    mixed_grad_ref,
    dense_ref,
):
    spots = spots_ref[...]
    rows = mm(spots, back_ref[...])
    gate_grad = jnp.zeros((TOK, 128), F32)
    for p in range(3):
        gate_grad += mm(spots * gate_rows_ref[p : p + 1, :], spread_ref[...])
    gates = gates_ref[...]
    chosen_grad = gates * (gate_grad - jnp.sum(gates * gate_grad, axis=-1, keepdims=True))
    logit_grad = chosen_grad.astype(BF)
    normed_grad = mm(logit_grad, small_ref[...], NT) + rows
    middle = middle_ref[...]
    inverse = lax.rsqrt(jnp.mean(middle * middle, axis=-1, keepdims=True) + EPSILON)
    hat = middle * inverse
    scaled = normed_grad * gains_ref[1:2, :]
    middle_grad = cot_ref[...].astype(F32) + inverse * (
        scaled - hat * jnp.mean(scaled * hat, axis=-1, keepdims=True)
    )
    middle_grad_ref[...] = middle_grad
    branch = middle_grad.astype(BF)
    mixed_grad = mm(branch, out_ref[...], NT).astype(BF)
    for g in range(NR):
        mixed_grad_ref[g] = mixed_grad[:, g * 128 : (g + 1) * 128]
    gain_grad = jnp.sum(normed_grad * hat, axis=0, keepdims=True)
    lane = lax.broadcasted_iota(jnp.int32, (D, 128), 1)
    gain_column = jnp.broadcast_to(gain_grad, (128, D)).T
    router_grad = mm(normed_ref[...], logit_grad, TN)
    dense_ref[:, D:] = jnp.where(lane == 32, gain_column, router_grad).astype(BF)
    for g in range(NR):
        dense_ref[g * 128 : (g + 1) * 128, :D] = mm(mixed_ref[g], branch, TN).astype(BF)


def token_back(back, spots, spread, gate_rows, gates, cot, middle, rows, gains, gathered, mixed):
    fixed = lambda count, width, at=0: pl.BlockSpec((count, width), lambda i: (0, at))
    return pl.pallas_call(
        token_kernel,
        grid=(1,),
        in_specs=[
            fixed(E * SLOTS, D),
            fixed(TOK, E * SLOTS),
            fixed(E * SLOTS, 128),
            fixed(3, E * SLOTS),
            fixed(TOK, 128),
            fixed(TOK, D),
            fixed(TOK, D),
            fixed(TOK, D),
            fixed(8, D),
            fixed(D, 128, 24),
            fixed(D, D, 2),
            pl.BlockSpec((NR, TOK, 128), lambda i: (0, 0, 0)),
        ],
        out_specs=[
            fixed(TOK, D),
            pl.BlockSpec((NR, TOK, 128), lambda i: (0, 0, 0)),
            fixed(D, D + 128),
        ],
        out_shape=[
            jax.ShapeDtypeStruct((TOK, D), F32),
            jax.ShapeDtypeStruct((NR, TOK, 128), BF),
            jax.ShapeDtypeStruct((D, D + 128), BF),
        ],
        compiler_params=pltpu.CompilerParams(vmem_limit_bytes=VMEM),
    )(back, spots, spread, gate_rows, gates, cot, middle, rows, gains, gathered, gathered, mixed)


def after(value, *others):
    return lax.optimization_barrier((value,) + others)[0]


def heads_kernel(parts_ref, query_ref, key_ref, value_ref, gain_ref, dq_ref, dk_ref, dv_ref, norm_ref):
    total = jnp.zeros((64, 128), F32)
    for pair in range(NR // 2):
        first, second = parts_ref[2 * pair, :64].astype(F32), parts_ref[2 * pair + 1, :64].astype(F32)
        lanes = slice(pair * 128, (pair + 1) * 128)
        for at, part in ((2 * pair, first), (2 * pair + 1, second)):
            wide = slice(at * 128, (at + 1) * 128)
            dq_ref[:, wide] = part[:, :128]
            total += part[:, :128] * query_ref[:, wide].astype(F32)
        dk = jnp.concatenate([first[:, 128:192], second[:, 128:192]], axis=1)
        dv = jnp.concatenate([first[:, 192:], second[:, 192:]], axis=1)
        dk_ref[:, lanes] = dk
        dv_ref[:, lanes] = dv
        total += dk * key_ref[:, lanes].astype(F32) + dv * value_ref[:, lanes].astype(F32)
    norm_ref[...] = jnp.sum(total, axis=1, keepdims=True) / gain_ref[...]


def finish_heads(parts, query_weight, key_matrix, value_matrix, norm_one):
    return pl.pallas_call(
        heads_kernel,
        out_shape=[
            jax.ShapeDtypeStruct((64, 1024), F32),
            jax.ShapeDtypeStruct((64, 512), F32),
            jax.ShapeDtypeStruct((64, 512), F32),
            jax.ShapeDtypeStruct((64, 1), F32),
        ],
    )(parts, query_weight, key_matrix, value_matrix, norm_one.astype(F32)[:, None])


def widen_kernel(places_ref, *refs):
    step = pl.program_id(0)
    out_ref = refs[-1]
    for n in range(places_ref.shape[0] // 2):

        @pl.when(step // 2 == n)
        def store(n=n):
            out_ref[...] = refs[n][...].astype(F32)


def widen(arrays, places, total=None):
    block = arrays[0].shape[0] // 2
    given = () if total is None else (total,)

    def taken(n):
        return pl.BlockSpec((block, FF), lambda i, places: (jnp.clip(i - 2 * n, 0, 1), 0))

    return pl.pallas_call(
        widen_kernel,
        grid_spec=pltpu.PrefetchScalarGridSpec(
            num_scalar_prefetch=1,
            grid=(2 * len(arrays),),
            in_specs=[taken(n) for n in range(len(arrays))]
            + [pl.BlockSpec(memory_space=pl.ANY)] * len(given),
            out_specs=pl.BlockSpec((block, FF), lambda i, places: (places[i], 0)),
        ),
        out_shape=jax.ShapeDtypeStruct((6 * D, FF), F32),
        input_output_aliases={1 + len(arrays): 0} if given else {},
    )(jnp.concatenate(places).astype(jnp.int32), *arrays, *given)


def exchange(x, bits, axis="replica"):
    return lax.ppermute(x, axis, [(i, i ^ bits) for i in range(lax.axis_size(axis))])


def halves(x, bit):
    half = x.shape[0] // 2
    take = lambda at: lax.dynamic_slice_in_dim(x, at * half, half, 0)
    return take(bit), take(1 - bit)


def in_order(own, other, bit):
    first = jnp.where(bit == 0, own, other)
    return jnp.concatenate([first, jnp.where(bit == 0, other, own)], axis=0)


def add_low(a, b):
    return (a.astype(F32) + b.astype(F32)).astype(BF)


def per_device(
    tokens,
    norm_one,
    query_weight,
    key_matrix,
    value_matrix,
    out_weight,
    norm_two,
    router,
    experts,
    routes,
    segments,
    cotangent,
):
    shard = lax.axis_index("shard")
    replica = lax.axis_index("replica")
    along_x = replica // 2
    side = replica % 2
    low_bit, high_bit = along_x % 2, along_x // 2
    mixed_bit = low_bit ^ high_bit

    grouped = jnp.concatenate(
        [
            query_weight.reshape(64, NR, 128),
            key_matrix.reshape(64, NR, HD),
            value_matrix.reshape(64, NR, HD),
        ],
        axis=2,
    ).reshape(64, 2048)
    small = jnp.concatenate(
        [router, norm_one[:, None], norm_two[:, None], jnp.zeros((64, 94), BF)], axis=1
    )
    gathered = lax.all_gather(
        jnp.concatenate([grouped, out_weight, small], axis=1), "shard", axis=0, tiled=True
    )

    segments_seq = spread_all(segments, "replica", NR).reshape(SEQ)
    first_segment = shard * 3
    count_one = jnp.sum((segments_seq == first_segment).astype(jnp.int32))
    count_two = jnp.sum((segments_seq == first_segment + 1).astype(jnp.int32))
    start = jnp.where(
        segments_seq == first_segment,
        0,
        jnp.where(segments_seq == first_segment + 1, count_one, count_one + count_two),
    ).reshape(NQ, 1, QB)

    chosen = jnp.any(routes[:, :, None] == jnp.arange(128, dtype=jnp.int32), axis=1)
    earlier = jnp.tril(jnp.ones((TOK, TOK), BF), -1)
    slot = jnp.where(chosen, mm(earlier, chosen.astype(BF)), -1.0)
    cot_rows = jnp.concatenate([cotangent, slot.astype(BF)], axis=1)
    cot_all = lax.all_gather(cot_rows, "shard", axis=0, tiled=True)
    spots = slot[:, :E, None] == jnp.arange(SLOTS, dtype=F32)
    spots = spots.astype(BF).reshape(TOK, E * SLOTS)
    spread = (
        jnp.arange(E * SLOTS)[:, None] // SLOTS == jnp.arange(128)[None, :]
    ).astype(BF)

    half = HD // 2
    frequency = 10000.0 ** (-2.0 * jnp.arange(half, dtype=F32) / HD)
    angles = jnp.arange(SEQ, dtype=F32)[:, None] * frequency[None, :]
    cosine, sine = jnp.cos(angles), jnp.sin(angles)
    cos_head = jnp.concatenate([cosine, cosine], axis=1)
    sin_head = jnp.concatenate([-sine, sine], axis=1)
    cos_here = lax.dynamic_slice(cos_head, (replica * TOK, 0), (TOK, HD))
    sin_here = lax.dynamic_slice(sin_head, (replica * TOK, 0), (TOK, HD))
    cos_group = jnp.concatenate(
        [cos_here * SCALE, cos_here * SCALE, cos_here, jnp.ones((TOK, HD), F32)], axis=1
    )
    sin_group = jnp.concatenate(
        [sin_here * SCALE, sin_here * SCALE, sin_here, jnp.zeros((TOK, HD), F32)], axis=1
    )

    tokens_in, start, spots, spread = lax.optimization_barrier((tokens, start, spots, spread))
    qkv_here, normed_one, gains = project(tokens_in, gathered, cos_group, sin_group)
    qkv = split_all(qkv_here, "replica").reshape(SEQ, 256)
    normed_one, qkv = lax.optimization_barrier((normed_one, qkv))
    normed_pair = in_order(normed_one, exchange(normed_one, 1), side)
    mixed_heads, lse = attend(qkv, start)
    mixed = split_all(mixed_heads.reshape(NR, TOK, 128), "replica")
    mixed, normed_pair = lax.optimization_barrier((mixed, normed_pair))
    normed_pairs = [normed_pair] + [exchange(normed_pair, 2 * k) for k in (1, 2, 3)]
    middle, rows_out, gates = route(mixed, tokens, gathered, gains, chosen.astype(F32))

    rows_all = lax.all_gather(rows_out, "shard", axis=0, tiled=True)
    normed_seq = jnp.concatenate(normed_pairs, axis=0)
    own_slots = lax.dynamic_slice(cot_all, (0, D + 2 * shard), (NS * TOK, 2)).astype(F32)
    own_slots = own_slots.T.reshape(2, CHUNKS, BLOCKS, TOK)
    lane = jnp.arange(128)[None, :]
    own = jnp.stack(
        [((lane % E == 2 * shard + e) & (lane < 3 * E)).astype(F32) for e in range(2)]
    )
    combined, grad_in, expert_grad = run_experts(rows_all, cot_all, own_slots, own, experts)
    back = split_all(after(grad_in, normed_seq), "shard")

    rows = expert_grad.reshape(2, 3 * D, FF)
    keep_a, send_a = halves(rows[0], mixed_bit)
    keep_b, send_b = halves(rows[1], high_bit)
    got_a, got_b = exchange(send_a, 2), exchange(send_b, 6)
    keep_a, send_a = halves(add_low(keep_a, got_a), low_bit)
    keep_b, send_b = halves(add_low(keep_b, got_b), low_bit)
    core, row, layer = shard % 2, shard // 2 % 2, shard // 4
    pick = lambda x, at: lax.dynamic_index_in_dim(x, at, 0, keepdims=False)
    for_core = pick(combined, 1 - core)
    back, send_a, send_b, for_core = lax.optimization_barrier((back, send_a, send_b, for_core))
    from_core = exchange(for_core, 1, "shard")
    got_a, got_b = exchange(send_a, 6), exchange(send_b, 2)

    gate_rows = back.reshape(E, SLOTS, D)[:, 60:63, :SLOTS].transpose(1, 0, 2).reshape(3, E * SLOTS)
    middle_grad, mixed_grad, dense = token_back(
        back.reshape(E * SLOTS, D),
        spots,
        spread,
        gate_rows,
        gates,
        cotangent,
        middle,
        rows_out,
        gains,
        gathered,
        mixed,
    )
    grad_heads = split_all(mixed_grad, "replica").reshape(SEQ, 128)
    grad_heads, got_a, got_b = lax.optimization_barrier((grad_heads, got_a, got_b))
    keep_a, send_a = halves(add_low(keep_a, got_a), side)
    keep_b, send_b = halves(add_low(keep_b, got_b), side)
    got = exchange(jnp.concatenate([send_a, send_b], axis=0), 1)
    head_grad = attend_back(
        qkv, grad_heads, start, lse, cosine.T, sine.T, cos_head, sin_head
    )
    head_grad, got = lax.optimization_barrier((head_grad, got))
    own = add_low(jnp.concatenate([keep_a, keep_b], axis=0), got)
    half = own.shape[0] // 2
    other = exchange(own, 1)
    head_rows = jnp.concatenate(
        [
            lax.dynamic_slice_in_dim(head_grad, (along_x ^ k) * 2 * TOK, 2 * TOK, 0)
            for k in range(4)
        ],
        axis=0,
    )
    heads_grad = mm(normed_seq, head_rows, TN).astype(BF)

    dense_parts = split_all(after(dense, grad_heads).reshape(NS, 64, 1152), "shard")
    dense_sum = jnp.sum(dense_parts.astype(F32), axis=0).astype(BF)
    dense_here = split_all(after(dense_sum, heads_grad).reshape(NR, 8, 1152), "replica")
    sums = add_low(pick(combined, core), after(from_core, heads_grad))
    keep = [[pick(sums[:, y], layer), pick(sums[:, y], layer ^ step)] for y, step in ((0, 3), (1, 1))]
    send = [
        jnp.stack([pick(sums[:, y], layer ^ first), pick(sums[:, y], layer ^ 2)])
        for y, first in ((0, 1), (1, 3))
    ]
    layers = [exchange(send[0], 4, "shard"), exchange(send[1], 12, "shard")]

    heads_grad, dense_here, other = lax.optimization_barrier((heads_grad, dense_here, other))
    heads_parts = split_all(heads_grad.reshape(NS, 64, 256), "shard")
    own_a = jnp.concatenate([own[:half], other[:half]], axis=0)
    own_b = jnp.concatenate([own[half:], other[half:]], axis=0)
    other_a, other_b = exchange(own_a, 6), exchange(own_b, 2)
    dense_total = jnp.sum(dense_here.astype(F32), axis=0).astype(BF)
    heads_sum = jnp.sum(heads_parts.astype(F32), axis=0).astype(BF)
    last = jnp.concatenate(
        [heads_sum, dense_total.reshape(36, 256), jnp.zeros((12, 256), BF)], axis=0
    )
    by_token = split_all(after(head_grad, heads_parts).reshape(NR, TOK, 256), "replica")
    next_a, next_b = exchange(after(own_a, heads_sum), 2), exchange(after(own_b, heads_sum), 6)
    by_token, other_a, other_b, *layers = lax.optimization_barrier(
        (by_token, other_a, other_b, *layers)
    )
    rest_a, rest_b = exchange(other_a, 2), exchange(other_b, 6)
    last = spread_all(after(last, by_token), "replica", NR)

    def places(first, bit, low):
        return first + 4 * bit + 2 * low + jnp.stack([side, 1 - side])

    expert_total = widen(
        [own_a, own_b, other_a, other_b, next_a, next_b],
        [
            places(0, mixed_bit, low_bit),
            places(8, high_bit, low_bit),
            places(0, mixed_bit, 1 - low_bit),
            places(8, high_bit, 1 - low_bit),
            places(0, 1 - mixed_bit, 1 - low_bit),
            places(8, 1 - high_bit, 1 - low_bit),
        ],
    )
    last, expert_total = lax.optimization_barrier((last, expert_total))
    keep = [[add_low(keep[y][n], layers[y][n]) for n in range(2)] for y in range(2)]
    layers = [exchange(keep[0][1], 12, "shard"), exchange(keep[1][1], 4, "shard")]
    query_grad, key_grad, value_grad, norm_one_grad = finish_heads(
        last, query_weight, key_matrix, value_matrix, norm_one
    )
    dense_last = last[:, 64:100].reshape(64, 1152).astype(F32)

    layers = [after(part, last) for part in layers]
    normed_grad = mm(by_token.transpose(1, 0, 2).reshape(TOK, 2048), gathered[:, :2048], NT)
    tokens_wide = tokens.astype(F32)
    inverse = lax.rsqrt(jnp.mean(tokens_wide * tokens_wide, axis=-1, keepdims=True) + EPSILON)
    hat = tokens_wide * inverse
    scaled = normed_grad * gains[0:1]
    tokens_grad = (
        middle_grad + inverse * (scaled - hat * jnp.mean(scaled * hat, axis=-1, keepdims=True))
    ).astype(BF)

    sides = [add_low(keep[y][0], layers[y]) for y in range(2)]
    own_side = jnp.where(row == 0, sides[0], sides[1])
    from_side = exchange(jnp.where(row == 0, sides[1], sides[0]), 2, "shard")
    from_side = after(from_side, tokens_grad)
    layer_out = (middle + own_side.astype(F32) + from_side.astype(F32)).astype(BF)
    expert_total = widen(
        [rest_a, rest_b],
        [places(0, 1 - mixed_bit, low_bit), places(8, 1 - high_bit, low_bit)],
        expert_total,
    )
    expert_total = expert_total.reshape(2, 3, D, FF)
    return (
        layer_out,
        tokens_grad,
        norm_one_grad[:, 0],
        query_grad,
        key_grad,
        value_grad,
        dense_last[:, :1024],
        dense_last[:, 1056],
        dense_last[:, 1024:1056],
        expert_total,
    )


def solution(mesh):
    return jax.shard_map(
        per_device,
        mesh=mesh,
        in_specs=(
            P(("shard", "replica"), None),
            P("shard"),
            P("shard", None),
            P("shard", None),
            P("shard", None),
            P("shard", None),
            P("shard"),
            P("shard", None),
            P("shard", None, None, None),
            P(("shard", "replica"), None),
            P(("shard", "replica")),
            P(("shard", "replica"), None),
        ),
        out_specs=(
            P(("shard", "replica"), None),
            P(("shard", "replica"), None),
            P("shard"),
            P("shard", None),
            P("shard", None),
            P("shard", None),
            P("shard", None),
            P("shard"),
            P("shard", None),
            P("shard", None, None, None),
        ),
        check_vma=False,
    )
```
